32 devices in a mesh: seq: 16 (over z, y, x), head: 2 (over core).
Axes of the slice: x: 2, y: 2, z: 4, core: 2. Of those that a mesh axis runs over, the one named last changes fastest.
Arguments:
- hidden: bfloat16 [4, 2048, 1152], P(None, ('seq', 'head')), may hold values from -6 to 6
- positions: int32 [4, 2048], P(None, ('seq', 'head')), may hold values from 0 to 2047, as said below
- input_gain: bfloat16 [1152], replicated, may hold values from 0.5 to 1.5
- query_weight: bfloat16 [1152, 1024], replicated, may hold values from -0.1875 to 0.1875
- key_weight: bfloat16 [1152, 256], replicated, may hold values from -0.1875 to 0.1875
- value_weight: bfloat16 [1152, 256], replicated, may hold values from -0.1875 to 0.1875
- query_gain: bfloat16 [256], replicated, may hold values from 0.5 to 1.5
- key_gain: bfloat16 [256], replicated, may hold values from 0.5 to 1.5
- out_weight: bfloat16 [1024, 1152], replicated, may hold values from -0.1875 to 0.1875
- branch_gain: bfloat16 [1152], replicated, may hold values from 0.5 to 1.5
- middle_gain: bfloat16 [1152], replicated, may hold values from 0.5 to 1.5
- gate_weight: bfloat16 [1152, 6912], P(None, 'head'), may hold values from -0.1875 to 0.1875
- up_weight: bfloat16 [1152, 6912], P(None, 'head'), may hold values from -0.1875 to 0.1875
- down_weight: bfloat16 [6912, 1152], P('head'), may hold values from -0.078125 to 0.078125
- final_gain: bfloat16 [1152], replicated, may hold values from 0.5 to 1.5
- cotangent: bfloat16 [4, 2048, 1152], P(None, ('seq', 'head')), may hold values from -6 to 6
Outputs:
- layer_output: bfloat16 [4, 2048, 1152], P(None, ('seq', 'head'))
- input_gradient: float32 [4, 2048, 1152], P(None, ('seq', 'head'))
- input_gain_gradient: float32 [1152], P(('seq', 'head'))
- query_gradient: float32 [1152, 1024], P(('seq', 'head'))
- key_gradient: float32 [1152, 256], P(('seq', 'head'))
- value_gradient: float32 [1152, 256], P(('seq', 'head'))
- query_gain_gradient: float32 [256], P(('seq', 'head'))
- key_gain_gradient: float32 [256], P(('seq', 'head'))
- out_gradient: float32 [1024, 1152], P(('seq', 'head'))
- branch_gain_gradient: float32 [1152], P(('seq', 'head'))
- middle_gain_gradient: float32 [1152], P(('seq', 'head'))
- gate_gradient: float32 [1152, 6912], P('seq', 'head')
- up_gradient: float32 [1152, 6912], P('seq', 'head')
- down_gradient: float32 [6912, 1152], P('head', 'seq')
- final_gain_gradient: float32 [1152], P(('seq', 'head'))
The draws below stay inside these ranges and needn't reach their ends.
Inputs may be any that keep to these rules, and one draw needn't show every extreme that they name: Each pack is a sequence of documents laid end to end, each covering whole aligned blocks of 1024 tokens; positions count from 0 at each document's first token. In every draw one pack, drawn from the seed, is a single document and another is cut at every block.
All inputs are finite; a program needn't handle non-finite values.
Results may differ from the reference program's by a relative error of at most 0.023.
Values may be sent and summed in bfloat16 or wider, within the bound.
No kernel may reach another device: no remote copies, remote signals or barrier semaphores. Data moves between devices by JAX's collectives and lax.ppermute only.
A program may use at most 384 MiB of HBM per device.

```python
import math
import jax
import jax.numpy as jnp
from jax import lax

D = 1152
HEADS = 4
HD = 256
FF = 6912
PACKS = 4
MIN_LEN = 1024
PACK_LEN = 2048


def draw_positions(key, part):
    key = jax.random.fold_in(key, 2)
    blocks_count = PACK_LEN // MIN_LEN
    whole_pack = jax.random.randint(jax.random.fold_in(key, 101), (), 0, PACKS)
    offset = jax.random.randint(jax.random.fold_in(key, 102), (), 1, PACKS)
    every_pack = (whole_pack + offset) % PACKS
    random_cuts = jax.random.randint(jax.random.fold_in(key, 103), (PACKS, blocks_count), 0, 2)
    pack_index = jnp.arange(PACKS, dtype=jnp.int32)[:, None]
    boundary = jnp.where(pack_index == whole_pack, 0, jnp.where(pack_index == every_pack, 1, random_cuts))
    block_index = jnp.arange(blocks_count, dtype=jnp.int32)[None, :]
    boundary = jnp.where(block_index == 0, 0, boundary)
    block_start = lax.cummax(jnp.where(boundary == 1, block_index, 0), axis=1)
    start_token = jnp.repeat(block_start * MIN_LEN, MIN_LEN, axis=1)
    token_index = jnp.arange(PACK_LEN, dtype=jnp.int32)[None, :]
    return (token_index - start_token).astype(jnp.int32)


def with_spikes(array, key, source, target, blocks, factor):
    def block_of(position):
        return (jnp.arange(array.shape[position]) // (array.shape[position] // blocks)).reshape((-1,) + (1,) * (array.ndim - 1 - position))

    near = jax.random.permutation(key, blocks)[block_of(target)]
    second = (block_of(target) + blocks // 2) % blocks
    return jnp.where((block_of(source) == near) | (block_of(source) == second), factor * array, array)


def block_scale(rng, extent, cuts, low, top_value):
    def one(position, parts):
        heights = jax.random.uniform(jax.random.fold_in(jax.random.fold_in(rng, 6), position), (parts,), jnp.float32, low / len(cuts), top_value / len(cuts))
        return jnp.repeat(jnp.exp(heights), extent[position] // parts).reshape((-1,) + (1,) * (len(extent) - position - 1))

    loudness = one(*cuts[0])
    for cut in cuts[1:]:
        loudness = loudness * one(*cut)
    return loudness


def noise(rng, dims, width, bound, shards=(), kind=jnp.bfloat16):
    level = block_scale(rng, dims, shards, -0.22, 0.18) if shards else 1.0
    entries = jax.random.normal(rng, dims, jnp.float32) * width * level
    return jnp.minimum(jnp.maximum(entries, -bound), bound).astype(kind)


def heavy_noise(rng, dims, deviation, reach, shards, heavy, kind=jnp.bfloat16):
    drawn = deviation * jax.random.normal(rng, dims, jnp.float32)
    if shards:
        drawn = drawn * block_scale(rng, dims, shards, -0.22, 0.18)
    return jnp.clip(with_spikes(drawn, jax.random.fold_in(rng, 3), *heavy), -reach, reach).astype(kind)


def setup_inputs(seed: int = 0) -> dict:
    key_list = jax.random.split(jax.random.key(seed), 17)
    return {
        "hidden": noise(key_list[0], (PACKS, PACK_LEN, D), 1.0, 6.0, ((1, 32),)),
        "positions": draw_positions(jax.random.fold_in(key_list[16], 71), 0),
        "input_gain": jnp.clip(1.0 + 0.1 * jax.random.normal(key_list[2], (D,), jnp.float32), 0.5, 1.5).astype(jnp.bfloat16),
        "query_weight": noise(key_list[3], (D, HEADS * HD), D ** -0.5, 0.1875),
        "key_weight": noise(key_list[4], (D, HD), D ** -0.5, 0.1875),
        "value_weight": noise(key_list[5], (D, HD), D ** -0.5, 0.1875),
        "query_gain": jnp.clip(1.0 + 0.1 * jax.random.normal(key_list[6], (HD,), jnp.float32), 0.5, 1.5).astype(jnp.bfloat16),
        "key_gain": jnp.clip(1.0 + 0.1 * jax.random.normal(key_list[7], (HD,), jnp.float32), 0.5, 1.5).astype(jnp.bfloat16),
        "out_weight": noise(key_list[8], (HEADS * HD, D), (HEADS * HD) ** -0.5, 0.1875),
        "branch_gain": jnp.clip(1.0 + 0.1 * jax.random.normal(key_list[9], (D,), jnp.float32), 0.5, 1.5).astype(jnp.bfloat16),
        "middle_gain": jnp.clip(1.0 + 0.1 * jax.random.normal(key_list[10], (D,), jnp.float32), 0.5, 1.5).astype(jnp.bfloat16),
        "gate_weight": noise(key_list[11], (D, FF), D ** -0.5, 0.1875, ((1, 2),)),
        "up_weight": noise(key_list[12], (D, FF), D ** -0.5, 0.1875, ((1, 2),)),
        "down_weight": noise(key_list[13], (FF, D), FF ** -0.5, 0.078125, ((0, 2),)),
        "final_gain": jnp.clip(1.0 + 0.1 * jax.random.normal(key_list[14], (D,), jnp.float32), 0.5, 1.5).astype(jnp.bfloat16),
        "cotangent": heavy_noise(key_list[15], (PACKS, PACK_LEN, D), 1.0, 6.0, ((1, 32),), (1, 2, 32, 2.75)),
    }


EPS = 1e-06
BASE = 1000000.0
HIGHEST = lax.Precision.HIGHEST

@jax.custom_vjp
def low(v):
    return lax.optimization_barrier(v.astype(jnp.bfloat16)).astype(jnp.float32)

@jax.custom_vjp
def low_back(v):
    return v

def low_keep(v):
    return (low(v), None)

def low_pass(kept, grad):
    return (grad,)

def back_keep(v):
    return (v, None)

def back_low(kept, grad):
    return (low(grad),)
low.defvjp(low_keep, low_pass)
low_back.defvjp(back_keep, back_low)

def normed(values, gain):
    return values * lax.rsqrt(lax.optimization_barrier(jnp.mean(values * values, -1, keepdims=True)) + EPS) * gain

def rotated(values, angles):
    half_size = values.shape[-1] // 2
    cosine = jnp.cos(angles)
    sine_part = jnp.sin(angles)
    first_half = values[..., :half_size]
    second_half = values[..., half_size:]
    return jnp.concatenate([first_half * cosine - second_half * sine_part, second_half * cosine + first_half * sine_part], -1)

def angles_for(positions, head_size):
    half_size = head_size // 2
    frequency = jnp.exp(jnp.arange(half_size, dtype=jnp.float32) * (-2.0 * math.log(BASE) / head_size))
    return positions.astype(jnp.float32)[..., None] * frequency

def product(left, right):
    return jnp.dot(left, right, precision=HIGHEST)

def attend(queries, key_rows, value_rows, positions):
    length = queries.shape[0]
    blocking = min(length, 1024)
    blocks_count = length // blocking
    scaling = queries.shape[-1] ** (-0.5)
    token_index = jnp.arange(length, dtype=jnp.int32)
    doc_start = (token_index - positions).astype(jnp.int32)

    @jax.checkpoint
    def one_block(element):
        block_query, block_start, block_index = element
        scores = low_back(jnp.einsum('rhd,nd->rhn', block_query, key_rows, precision=HIGHEST) * scaling)
        allowed = (token_index[None, :] >= block_start[:, None]) & (token_index[None, :] <= block_index[:, None])
        exponent = jnp.where(allowed[:, None, :], jnp.exp(scores), 0.0)
        totals = lax.optimization_barrier(jnp.sum(exponent, -1))
        numerator = low_back(jnp.einsum('rhn,nd->rhd', low(exponent), value_rows, precision=HIGHEST))
        return numerator / totals[..., None]
    head_count = queries.shape[1]
    head_size = queries.shape[2]
    pieces = (queries.reshape(blocks_count, blocking, head_count, head_size), doc_start.reshape(blocks_count, blocking), token_index.reshape(blocks_count, blocking))
    return lax.map(one_block, pieces).reshape(length, head_count, head_size)

def one_pack(element, params):
    tokens, positions = element
    input_gain, query_weight, key_weight, value_weight, query_gain, key_gain, out_weight, branch_gain, middle_gain, gate_weight, up_weight, down_weight, final_gain = params
    length = tokens.shape[0]
    head_size = key_weight.shape[1]
    head_count = query_weight.shape[1] // head_size
    angles = angles_for(positions, head_size)
    normed_input = low(normed(tokens, input_gain))
    query_raw = low_back(product(normed_input, query_weight)).reshape(length, head_count, head_size)
    key_raw = low_back(product(normed_input, key_weight))
    value_rows = low_back(low(product(normed_input, value_weight)))
    queries = low_back(low(rotated(normed(query_raw, query_gain), angles[:, None, :])))
    key_rows = low_back(low(rotated(normed(key_raw, key_gain), angles)))
    attended = attend(queries, key_rows, value_rows, positions)
    mixed = low_back(low(attended.reshape(length, head_count * head_size)))
    branch = low_back(product(mixed, out_weight))
    residual = tokens + normed(branch, branch_gain)
    middle = low(normed(residual, middle_gain))
    gate = low_back(product(middle, gate_weight))
    upward = low_back(product(middle, up_weight))
    activated = low(jax.nn.gelu(gate, approximate=True) * upward)
    feed = low_back(product(activated, down_weight))
    return residual + normed(feed, final_gain)

def reference(hidden, positions, input_gain, query_weight, key_weight, value_weight, query_gain, key_gain, out_weight, branch_gain, middle_gain, gate_weight, up_weight, down_weight, final_gain, cotangent):
    weights = (input_gain.astype(jnp.float32), query_weight.astype(jnp.float32), key_weight.astype(jnp.float32), value_weight.astype(jnp.float32), query_gain.astype(jnp.float32), key_gain.astype(jnp.float32), out_weight.astype(jnp.float32), branch_gain.astype(jnp.float32), middle_gain.astype(jnp.float32), gate_weight.astype(jnp.float32), up_weight.astype(jnp.float32), down_weight.astype(jnp.float32), final_gain.astype(jnp.float32))
    tokens = hidden.astype(jnp.float32)

    def layer(tokens_in, input_g, query_w, key_w, value_w, query_g, key_g, out_w, branch_g, middle_g, gate_w, up_w, down_w, final_g):
        params = (input_g, query_w, key_w, value_w, query_g, key_g, out_w, branch_g, middle_g, gate_w, up_w, down_w, final_g)
        return lax.map(jax.checkpoint(lambda element: one_pack(element, params)), (tokens_in, positions))
    result, pullback = jax.vjp(layer, tokens, weights[0], weights[1], weights[2], weights[3], weights[4], weights[5], weights[6], weights[7], weights[8], weights[9], weights[10], weights[11], weights[12])
    grads = pullback(cotangent.astype(jnp.float32))
    return (result.astype(jnp.bfloat16), grads[0], grads[1], grads[2], grads[3], grads[4], grads[5], grads[6], grads[7], grads[8], grads[9], grads[10], grads[11], grads[12], grads[13])
```

```python
import functools
import math

import jax
import jax.numpy as jnp
from jax import lax
from jax.experimental import pallas as pl
from jax.experimental.pallas import tpu as pltpu
from jax.sharding import Mesh, PartitionSpec as P

EPS = 1e-06
BASE = 1000000.0
BF = jnp.bfloat16
F32 = jnp.float32
LANES = 128
MEGA = 1024 * 1024
FEED_TILE, LIST_TILE = 512, 1024
VMEM = 56 * MEGA
WHOLE_ROOM, TILE_ROOM = 56 * MEGA, 56 * MEGA
SMALL = pl.CostEstimate(flops=1, bytes_accessed=1, transcendentals=0)


def normed(values, gain):
    return values * lax.rsqrt(jnp.mean(values * values, -1, keepdims=True) + EPS) * gain


def normed_back(values, gain, grad):
    scale = lax.rsqrt(jnp.mean(values * values, -1, keepdims=True) + EPS)
    pull = grad * gain
    shared = jnp.mean(values * pull, -1, keepdims=True) * (scale * scale * scale)
    return scale * pull - values * shared, jnp.sum(grad * values * scale, 0, keepdims=True)


def turned(values, cosine, sine, way):
    half = values.shape[-1] // 2
    first, second = values[:, :half], values[:, half:]
    return jnp.concatenate([first * cosine - way * second * sine, second * cosine + way * first * sine], -1)


def angles_for(positions, head_size):
    half_size = head_size // 2
    frequency = jnp.exp(
        jnp.arange(half_size, dtype=jnp.float32) * (-2.0 * math.log(BASE) / head_size)
    )
    return positions.astype(jnp.float32)[..., None] * frequency


def dot(left, right):
    return jnp.dot(left, right, preferred_element_type=F32)


def dot_nt(left, right):
    return lax.dot_general(left, right, (((1,), (1,)), ((), ())), preferred_element_type=F32)


def dot_tn(left, right):
    return lax.dot_general(left, right, (((0,), (0,)), ((), ())), preferred_element_type=F32)


def bits_of(count):
    return count.bit_length() - 1


DOWN, GATE, UP = 0, 10, 20
OUT, QUERY, PAIR, PAIRS = range(30, 34)
BACK, BRANCH, ATTEND, QUERY_LISTS, PAIR_LISTS, INPUT = range(40, 46)
SEND_MIDDLE, SEND_GRAD, SEND_PAIR = range(50, 53)
JOINT = 60
ALONG_X, ALONG_Y, NEAR, FAR = range(4)
DOWN_CUTS = (2, 2)
GATE_CUTS = (2, 2)
UP_CUTS = (1, 1, 2)
ORDERS = {
    DOWN: (ALONG_X, ALONG_Y),
    DOWN + 1: (ALONG_Y, ALONG_X),
    GATE: (ALONG_Y, ALONG_X, NEAR, FAR),
    GATE + 1: (ALONG_X, ALONG_Y, NEAR, FAR),
    UP: (ALONG_X, ALONG_Y, NEAR, FAR),
    UP + 1: (ALONG_Y, ALONG_X, NEAR, FAR),
    UP + 2: (NEAR, ALONG_X, ALONG_Y, FAR),
    OUT: (ALONG_X, ALONG_Y),
    QUERY: (ALONG_Y, ALONG_X),
    PAIR: (ALONG_Y, ALONG_X),
}
STEPS = {DOWN: 2, DOWN + 1: 2, GATE: 2, GATE + 1: 2, UP: 2, UP + 1: 2, UP + 2: 4, OUT: 2, QUERY: 2, PAIR: 2}
JOINTS = {
    JOINT: ((DOWN, DOWN + 1), ()),
    JOINT + 1: ((GATE, GATE + 1), (NEAR, FAR)),
    JOINT + 2: ((UP, UP + 1), (NEAR, FAR)),
}
DOWN_RESULT = (JOINT,)
GATE_RESULT = (JOINT + 1,)
UP_RESULT = (JOINT + 2, UP + 2)
WORK, SEND, TAKE, START, LAND, END = range(6)
PLAN = (
    (WORK, DOWN),
    (START, DOWN + 1),
    (START, DOWN),
    (WORK, BACK),
    (SEND, SEND_MIDDLE),
    (WORK, GATE),
    (START, GATE + 1),
    (START, GATE),
    (WORK, UP),
    (TAKE, SEND_MIDDLE),
    (WORK, BRANCH),
    (START, UP + 2),
    (LAND, DOWN + 1),
    (LAND, DOWN),
    (START, DOWN),
    (WORK, OUT),
    (WORK, ATTEND),
    (START, DOWN + 1),
    (START, OUT),
    (LAND, GATE + 1),
    (LAND, GATE),
    (START, UP + 1),
    (START, GATE + 1),
    (SEND, SEND_GRAD),
    (START, UP),
    (LAND, DOWN + 1),
    (START, GATE),
    (LAND, DOWN),
    (END, PAIRS),
    (LAND, OUT),
    (TAKE, SEND_GRAD),
    (WORK, PAIR),
    (SEND, SEND_PAIR),
    (WORK, QUERY),
    (LAND, UP + 2),
    (LAND, UP + 1),
    (LAND, GATE),
    (WORK, QUERY_LISTS),
    (TAKE, SEND_PAIR),
    (START, QUERY),
    (START, UP + 2),
    (START, OUT),
    (LAND, GATE + 1),
    (WORK, PAIR_LISTS),
    (START, PAIR),
    (START, JOINT + 1),
    (LAND, QUERY),
    (LAND, UP),
    (START, UP),
    (LAND, OUT),
    (LAND, PAIR),
    (START, UP + 1),
    (LAND, UP + 2),
    (END, JOINT),
    (START, PAIR),
    (START, UP + 2),
    (LAND, JOINT + 1),
    (START, JOINT + 1),
    (LAND, PAIR),
    (START, QUERY),
    (LAND, UP),
    (LAND, UP + 2),
    (WORK, INPUT),
    (LAND, UP + 1),
    (START, JOINT + 2),
    (START, UP + 2),
    (LAND, JOINT + 1),
    (LAND, QUERY),
    (LAND, JOINT + 2),
    (START, JOINT + 2),
    (END, OUT),
    (LAND, UP + 2),
    (LAND, JOINT + 2),
    (TAKE, INPUT),
    (END, PAIR),
    (END, QUERY),
)

GROUPS = ("far", "near")


def exchanged(value, mask, axis="quad"):
    count = lax.axis_size(axis)
    return lax.ppermute(value, axis, [(i, i ^ mask) for i in range(count)])


def shifted(value, step):
    count = lax.axis_size(GROUPS)
    return lax.ppermute(value, GROUPS, [(i, i + step) for i in range(count) if 0 <= i + step < count])


def over_head(value):
    return lax.ppermute(value, "head", [(0, 1), (1, 0)])


def over_step(value, step):
    if step in (NEAR, FAR):
        return exchanged(value, 1, GROUPS[1] if step == NEAR else GROUPS[0])
    return exchanged(value, 1 << step)


def to_packs(value, place):
    pieces = [lax.dynamic_index_in_dim(value, place, 0, False)]
    for mask in range(1, value.shape[0]):
        pieces.append(exchanged(lax.dynamic_index_in_dim(value, place ^ mask, 0, False), mask))
    return pieces


def from_packs(value, packs):
    rows = value.shape[0] // packs
    pieces = [value[mask * rows : (mask + 1) * rows] for mask in range(packs)]
    return [pieces[0]] + [exchanged(pieces[mask], mask) for mask in range(1, packs)]


def in_place(pieces, place):
    blocks = jnp.stack(pieces).reshape((2, 2) + pieces[0].shape)
    blocks = jnp.where(place & 1 == 1, jnp.flip(blocks, 1), blocks)
    blocks = jnp.where(place & 2 == 2, jnp.flip(blocks, 0), blocks)
    return blocks.reshape((len(pieces),) + pieces[0].shape)


def tie(token, *values):
    result = lax.optimization_barrier((token,) + values)
    return result


def list_places(order, packs, far_count):
    sizes = {ALONG_X: 2, ALONG_Y: 2, NEAR: 2, FAR: far_count}
    own = {NEAR: lax.axis_index("near"), FAR: lax.axis_index("far")}
    own[ALONG_X], own[ALONG_Y] = lax.axis_index("quad") & 1, lax.axis_index("quad") >> 1
    rest = jnp.arange(2 * packs * far_count, dtype=jnp.int32)
    at = {}
    for step in reversed(tuple(order) + tuple(step for step in (FAR, NEAR) if step not in order)):
        digit = rest % sizes[step]
        at[step] = digit ^ own[step] if step in order and sizes[step] == 2 else digit
        rest = rest // sizes[step]
    return ((at[FAR] * 2 + at[NEAR]) * packs + at[ALONG_Y] * 2 + at[ALONG_X]).astype(jnp.int32)


class Chain:
    def __init__(self, lists, order, last=False):
        self.keep, self.send = lists
        self.order = order
        self.last = last
        self.stage = 0
        self.rest = None

    def whole(self):
        return self.order[self.stage] == FAR and lax.axis_size("far") > 2

    def start(self, token):
        if not self.whole():
            token, send = tie(token, self.send)
            self.flight = over_step(send, self.order[self.stage])
        return token

    def land(self, token):
        if self.whole():
            total = summed_over(jnp.concatenate([self.keep, self.send], 0), "far")
            self.stage += 1
            if self.stage == len(self.order):
                self.rest = total.astype(F32)
            else:
                self.keep, self.send = halves(total)
            return token
        token, arrived, keep = tie(token, self.flight, self.keep)
        self.stage += 1
        if self.stage == len(self.order):
            total = keep.astype(F32) + arrived.astype(F32)
            token, self.rest = tie(token, total if self.last else total.astype(BF))
            return token
        half = keep.shape[0] // 2
        send = (keep[half:].astype(F32) + arrived[half:].astype(F32)).astype(BF)
        keep = (keep[:half].astype(F32) + arrived[:half].astype(F32)).astype(BF)
        token, self.keep, self.send = tie(token, keep, send)
        return token


def halves(total):
    half = total.shape[0] // 2
    return total[:half], total[half:]


def summed_over(value, axes):
    return lax.psum_scatter(value, axes, scatter_dimension=0, tiled=True)


def allowed_mask(info, rows, packs, length):
    group, place, head, start = info[0], info[1], info[2], info[3]
    span = rows * packs
    column = lax.broadcasted_iota(jnp.int32, (1, length), 1)
    chip = (group - column // span) * packs + ((column % span) // rows ^ place)
    key_index = (chip * 2 + head) * rows + column % rows
    row = lax.broadcasted_iota(jnp.int32, (2 * span, 1), 0)
    chip = group * packs + ((row % span) // rows ^ place)
    query_index = (chip * 2 + row // span) * rows + row % rows
    return (key_index >= start) & (key_index <= query_index)


def attend_kernel(heads, rows, packs, groups, info, queries, *refs):
    pairs, (out,) = refs[:groups], refs[groups:]
    size = queries.shape[1] // heads
    keys = jnp.concatenate([ref[:, :size] for ref in pairs], 0)
    values = jnp.concatenate([ref[:, size:] for ref in pairs], 0)
    allowed = allowed_mask(info, rows, packs, keys.shape[0])
    lane = lax.broadcasted_iota(jnp.int32, (queries.shape[0], LANES), 1)
    lanes = jnp.zeros(lane.shape, F32)
    for h in range(heads):
        cut = slice(h * size, (h + 1) * size)
        expo = jnp.where(allowed, jnp.exp(dot_nt(queries[:, cut], keys)), 0.0)
        totals = jnp.sum(expo, -1, keepdims=True)
        out[:, cut] = dot(expo.astype(BF), values).astype(BF)
        high = totals.astype(BF).astype(F32)
        lanes = jnp.where(lane == h, high, jnp.where(lane == heads + h, totals - high, lanes))
    out[:, heads * size :] = lanes.astype(BF)


def attend_back_kernel(heads, rows, packs, groups, info, queries, grads, *refs):
    pairs, (query_out, pair_out) = refs[:groups], refs[groups:]
    span = rows * packs
    size = queries.shape[1] // heads
    keys = jnp.concatenate([ref[:, :size] for ref in pairs], 0)
    values = jnp.concatenate([ref[:, size:] for ref in pairs], 0)
    allowed = allowed_mask(info, rows, packs, keys.shape[0])
    key_grad = jnp.zeros(keys.shape, F32)
    value_grad = jnp.zeros(keys.shape, F32)
    lanes = grads[:, heads * size :].astype(F32)
    for h in range(heads):
        cut = slice(h * size, (h + 1) * size)
        query, grad = queries[:, cut], grads[:, cut]
        delta = lanes[:, h : h + 1] + lanes[:, heads + h : heads + h + 1]
        expo = jnp.where(allowed, jnp.exp(dot_nt(query, keys)), 0.0)
        score_grad = (expo * (dot_nt(grad, values) - delta)).astype(BF)
        query_out[:, cut] = (dot(score_grad, keys) * (size**-0.5)).astype(BF)
        key_grad = key_grad + dot_tn(score_grad, query)
        value_grad = value_grad + dot_tn(expo.astype(BF), grad)
    both = jnp.concatenate([key_grad, value_grad], 1).astype(BF)
    for index in range(groups):
        target = lax.rem(info[0] - index + groups, groups) * span
        pair_out[pl.ds(pl.multiple_of(target, span), span), :] = both[index * span : (index + 1) * span]


def room(args, outs, scratch):
    sizes = [math.prod(one.shape) * one.dtype.itemsize for one in args]
    sizes += [math.prod(shape) * jnp.dtype(kind).itemsize for shape, kind in outs]
    sizes += [math.prod(one.shape) * jnp.dtype(one.dtype).itemsize for one in scratch]
    return min(VMEM, sum(sizes) + max(sum(sizes), WHOLE_ROOM))


def whole_call(kernel, outs, *args, scratch=()):
    spec = pl.BlockSpec(memory_space=pltpu.VMEM)
    return pl.pallas_call(
        kernel,
        in_specs=[pl.BlockSpec(memory_space=pltpu.SMEM)] + [spec] * (len(args) - 1),
        out_specs=[spec] * len(outs),
        out_shape=[jax.ShapeDtypeStruct(*out) for out in outs],
        scratch_shapes=list(scratch),
        cost_estimate=SMALL,
        compiler_params=pltpu.CompilerParams(vmem_limit_bytes=room(args[1:], outs, scratch)),
    )(*args)


def attend(info, queries, pairs, heads, packs):
    tokens, width = queries.shape
    kernel = functools.partial(attend_kernel, heads, tokens // 2 // packs, packs, len(pairs))
    return whole_call(kernel, [((tokens, width + LANES), BF)], info, queries, *pairs)[0]


def attend_back(info, queries, grads, pairs, heads, packs):
    tokens, width = queries.shape
    outs = [((tokens, width), BF), ((len(pairs) * tokens // 2, pairs[0].shape[1]), BF)]
    kernel = functools.partial(attend_back_kernel, heads, tokens // 2 // packs, packs, len(pairs))
    return whole_call(kernel, outs, info, queries, grads, *pairs)


def own_rows(info, ref):
    span = ref.shape[0] // 2
    return ref[pl.ds(pl.multiple_of(info[2] * span, span), span), :]


def by_core(info, own, other):
    lower = info[2] == 0
    return jnp.concatenate([jnp.where(lower, own, other), jnp.where(lower, other, own)], 0)


def sum_of(part, arrived):
    return part[...].astype(F32) + arrived[...].astype(F32)


def enter_kernel(count, info, *refs):
    pieces = refs[:count]
    gain, key_w, value_w, key_gain, cosine, sine, tokens_out, raw_out, pair_out = refs[count:]
    tokens = jnp.concatenate([piece[...] for piece in pieces], 0)
    tokens_out[...] = tokens
    rows = normed(tokens.astype(F32), gain[...]).astype(BF)
    raw = dot(rows, key_w[...])
    raw_out[...] = raw
    size = raw.shape[1]
    turn = turned(normed(raw, key_gain[...]), own_rows(info, cosine), own_rows(info, sine), 1.0)
    pair_out[:, :size] = turn.astype(BF)
    pair_out[:, size:] = dot(rows, value_w[...]).astype(BF)


def query_kernel(heads, info, own, other, gain, query_w, query_gain, cosine, sine, *outs):
    tokens_out, normed_out, raw_out, query_out = outs
    tokens = by_core(info, own[...], other[...])
    tokens_out[...] = tokens
    rows = normed(tokens.astype(F32), gain[...]).astype(BF)
    normed_out[...] = rows
    raw = dot(rows, query_w[...])
    raw_out[...] = raw
    size = raw.shape[1] // heads
    for h in range(heads):
        cut = slice(h * size, (h + 1) * size)
        turn = turned(normed(raw[:, cut], query_gain[...]), cosine[...], sine[...], 1.0).astype(BF)
        query_out[:, cut] = (turn.astype(F32) * (size**-0.5)).astype(BF)


def branch_kernel(heads, info, part, arrived, tokens, out_w, branch_gain, middle_gain, *outs):
    attended_out, total_out, mixed_out, branch_out, residual_out, middle_out = outs
    width = attended_out.shape[1]
    size = width // heads
    lanes = sum_of(part.at[:, width:], arrived.at[:, width:])
    lane = lax.broadcasted_iota(jnp.int32, lanes.shape, 1)
    totals = jnp.zeros(lanes.shape, F32)
    for h in range(heads):
        cut = slice(h * size, (h + 1) * size)
        total = lanes[:, h : h + 1] + lanes[:, heads + h : heads + h + 1]
        attended = sum_of(part.at[:, cut], arrived.at[:, cut]) / total
        attended_out[:, cut] = attended
        mixed_out[:, cut] = attended.astype(BF)
        totals = jnp.where(lane == h, total, totals)
    total_out[...] = totals
    branch = dot(mixed_out[...], out_w[...])
    branch_out[...] = branch
    residual = tokens[...].astype(F32) + normed(branch, branch_gain[...])
    residual_out[...] = residual
    middle_out[...] = normed(residual, middle_gain[...]).astype(BF)


def finish_kernel(info, part, arrived, residual, own, other, gain, output, upstream_out, grad_out, gain_out, rows):
    upstream = by_core(info, own[...], other[...])
    upstream_out[...] = upstream
    feed = sum_of(part, arrived)
    rows[...] = residual[...] + normed(feed, gain[...])
    output[...] = own_rows(info, rows).astype(BF)
    grad, gain_grad = normed_back(feed, gain[...], upstream.astype(F32))
    grad_out[...] = grad.astype(BF)
    gain_out[...] = 0.5 * gain_grad


def branch_back_kernel(heads, info, part, arrived, residual, branch, upstream, attended, totals, out_w, *refs):
    middle_gain, branch_gain, grad_out, half_out, scaled_out, middle_sum, branch_sum = refs
    part, gain_grad = normed_back(residual[...], middle_gain[...], sum_of(part, arrived))
    middle_sum[...] = 0.5 * gain_grad
    residual_grad = upstream[...].astype(F32) + part
    grad_out[...] = residual_grad
    branch_grad, gain_grad = normed_back(branch[...], branch_gain[...], residual_grad)
    branch_sum[...] = 0.5 * gain_grad
    low = branch_grad.astype(BF)
    half = half_out.shape[1]
    half_out[...] = jnp.where(info[2] == 0, low[:, :half], low[:, low.shape[1] - half :])
    mixed_grad = dot_nt(low, out_w[...]).astype(BF).astype(F32)
    width = mixed_grad.shape[1]
    size = width // heads
    lane = lax.broadcasted_iota(jnp.int32, (low.shape[0], LANES), 1)
    lanes = jnp.zeros(lane.shape, F32)
    for h in range(heads):
        cut = slice(h * size, (h + 1) * size)
        total = totals[:, h : h + 1]
        scaled_out[:, cut] = (mixed_grad[:, cut] / total).astype(BF)
        delta = jnp.sum(mixed_grad[:, cut] * attended[:, cut], -1, keepdims=True) / total
        high = delta.astype(BF).astype(F32)
        lanes = jnp.where(lane == h, high, jnp.where(lane == heads + h, delta - high, lanes))
    scaled_out[:, width:] = lanes.astype(BF)


def query_back_kernel(heads, info, part, arrived, raw, gain, cosine, sine, query_w, half_out, sum_out, back_out, low):
    size = raw.shape[1] // heads
    gain_sum = jnp.zeros((1, size), F32)
    for h in range(heads):
        cut = slice(h * size, (h + 1) * size)
        grad = sum_of(part.at[:, cut], arrived.at[:, cut]).astype(BF).astype(F32)
        grad, more = normed_back(raw[:, cut], gain[...], turned(grad, cosine[...], sine[...], -1.0))
        low[:, cut] = grad.astype(BF)
        gain_sum = gain_sum + more
    sum_out[...] = 0.5 * gain_sum
    half = half_out.shape[1]
    half_out[...] = jnp.where(info[2] == 0, low[:, :half], low[:, half:])
    back_out[...] = dot_nt(own_rows(info, low), query_w[...])


def key_back_kernel(info, pair_grad, raw, gain, cosine, sine, mine_out, other_out, low_out, sum_out):
    size = raw.shape[1]
    turned_grad = turned(pair_grad[:, :size].astype(F32), own_rows(info, cosine), own_rows(info, sine), -1.0)
    grad, sum_out[...] = normed_back(raw[...], gain[...], turned_grad)
    low, value = grad.astype(BF), pair_grad[:, size:]
    low_out[:, :size] = low
    low_out[:, size:] = value
    lower = info[2] == 0
    mine_out[...] = jnp.where(lower, low, value)
    other_out[...] = jnp.where(lower, value, low)


def leave_kernel(info, back, low, key_w, value_w, tokens, gain, residual_grad, output, rows_out):
    size, width = key_w.shape[1], tokens.shape[1]
    rows_out[:, width:] = output[...]
    grad = back[...] + dot_nt(low[:, :size], key_w[...]) + dot_nt(low[:, size:], value_w[...])
    part, ignored = normed_back(tokens[...].astype(F32), gain[...], grad)
    rows_out[:, :width] = (own_rows(info, residual_grad) + part).astype(BF)


def feed_kernel(rest, rows, gate_w, up_w, down_w, act_out, gate_out, up_out, feed_out, total):
    step = pl.program_id(0)
    last = pl.num_programs(0) - 1

    @pl.when(step == 0)
    def begin():
        total[...] = jnp.zeros_like(total)

    def tile(size):
        gate = dot(rows[...], gate_w[:, :size])
        upward = dot(rows[...], up_w[:, :size])
        root = math.sqrt(2.0 / math.pi)
        square = gate * gate
        bend = jnp.tanh(gate * (root + (root * 0.044715) * square))
        half = 0.5 + 0.5 * bend
        gelu = gate * half
        slope = half + (0.5 * gate) * (1.0 - bend * bend) * (root + (3 * 0.044715 * root) * square)
        act = (gelu * upward).astype(BF)
        act_out[:, :size] = act
        gate_out[:, :size] = (slope * upward).astype(BF)
        up_out[:, :size] = gelu.astype(BF)
        total[...] += dot(act, down_w[:size])

    pl.when(step < last)(lambda: tile(gate_w.shape[1]))
    pl.when(step == last)(lambda: tile(rest))

    @pl.when(step == last)
    def finish():
        feed_out[...] = total[...].astype(BF)


def steps_of(length, tile):
    steps = -(-length // tile)
    return steps, length - (steps - 1) * tile


def fixed(shape):
    return pl.BlockSpec(shape, lambda i, *_: (0,) * len(shape))


def columns(rows, tile):
    return pl.BlockSpec((rows, tile), lambda i, *_: (0, i))


def feed_forward(rows, gate_w, up_w, down_w):
    tokens, width = rows.shape
    hidden = gate_w.shape[1]
    tile = FEED_TILE
    steps, rest = steps_of(hidden, tile)
    return pl.pallas_call(
        functools.partial(feed_kernel, rest),
        grid=(steps,),
        in_specs=[
            fixed((tokens, width)),
            columns(width, tile),
            columns(width, tile),
            pl.BlockSpec((tile, width), lambda i: (i, 0)),
        ],
        out_specs=[columns(tokens, tile)] * 3 + [fixed((tokens, width))],
        out_shape=[jax.ShapeDtypeStruct((tokens, hidden), BF)] * 3 + [jax.ShapeDtypeStruct((tokens, width), BF)],
        scratch_shapes=[pltpu.VMEM((tokens, width), F32)],
        cost_estimate=SMALL,
        compiler_params=pltpu.CompilerParams(vmem_limit_bytes=TILE_ROOM),
    )(rows, gate_w, up_w, down_w)


def put_lists(left, plain, listed, low, places, count, orders):
    plain[...] = left[...].astype(F32).T
    block = plain.shape[0] // count
    for which in range(orders):
        for entry in range(count):
            first = places[which * count + entry] * block
            if block % 8 == 0:
                first = pl.multiple_of(first, 8)
            listed[entry * block : (entry + 1) * block, :] = plain[pl.ds(first, block), :]
        low[which] = listed[...].astype(BF)


def lists_outside(places, left):
    blocks = left.T.reshape(places.shape[1], -1, left.shape[0])
    return jnp.stack([jnp.take(blocks, place, axis=0).reshape(left.shape[1], -1) for place in places])


def emit(result, outs):
    if len(outs) == 1:
        outs[0][...] = result
    else:
        half = result.shape[0] // 2
        outs[0][...] = result[:half]
        outs[1][...] = result[half:]


def span_spec(rows, tile, first, last):
    return pl.BlockSpec((rows, tile), lambda i, *_: (0, jnp.clip(i - first, 0, last - first - 1)))


def wgrad_kernel(count, orders, route, cuts, inside, places, left, right, *refs):
    step = pl.program_id(0)
    outs, (plain, listed, low) = refs[:-3], refs[-3:]

    @pl.when(step == 0)
    def begin():
        if inside:
            put_lists(left, plain, listed, low, places, count, orders)
        else:
            low[...] = left[...]

    for index, (order, first, last) in enumerate(route):

        @pl.when((step >= first) & (step < last))
        def piece(index=index, order=order):
            emit(dot(low[order], right[...]).astype(BF), outs[cuts[index][0] : cuts[index][1]])


def weight_lists(places, left, right, route, tile):
    tokens, width = left.shape
    orders, count = places.shape
    steps, ignored = steps_of(right.shape[1], tile)
    outs, specs, cuts = [], [], []
    for ignored, first, last in route:
        cuts.append((len(outs), len(outs) + 2))
        for ignored in range(2):
            outs.append(jax.ShapeDtypeStruct((width // 2, min(last * tile, right.shape[1]) - first * tile), BF))
            specs.append(span_spec(width // 2, tile, first, last))
    inside = width // count % 8 == 0
    given = left if inside else lists_outside(places, left)
    plain = (width, tokens) if inside else (8, LANES)
    result = pl.pallas_call(
        functools.partial(wgrad_kernel, count, orders, route, cuts, inside),
        grid_spec=pltpu.PrefetchScalarGridSpec(
            num_scalar_prefetch=1,
            grid=(steps,),
            in_specs=[fixed(given.shape), columns(tokens, tile)],
            out_specs=specs,
            scratch_shapes=[
                pltpu.VMEM(plain, F32),
                pltpu.VMEM(plain, F32),
                pltpu.VMEM((orders, width, tokens), BF),
            ],
        ),
        out_shape=outs,
        cost_estimate=SMALL,
        compiler_params=pltpu.CompilerParams(vmem_limit_bytes=TILE_ROOM),
    )(places.reshape(-1), given, right)
    return [result[first:last] for first, last in cuts]


def small_lists_kernel(count, inside, rights, with_sums, places, left, *refs):
    right = refs[0][...]
    if rights == 2:
        lower = places[count] == 0
        other = refs[1][...]
        right = jnp.concatenate([jnp.where(lower, right, other), jnp.where(lower, other, right)], 0)
    refs = refs[rights:]
    given, (keep, send), (plain, listed, low, sums, sums_low) = refs[:-7], refs[-7:-5], refs[-5:]
    if inside:
        put_lists(left, plain, listed, low, places, count, 1)
    else:
        low[...] = left[...]
    wide = right.shape[1]
    half = low.shape[1] // 2
    result = dot(low[0], right).astype(BF)
    keep[:, :wide] = result[:half]
    send[:, :wide] = result[half:]
    if not with_sums:
        return
    if inside:
        rows = [one[...] for one in given]
        rows.append(jnp.zeros((LANES - len(rows), rows[0].shape[1]), F32))
        sums[...] = jnp.concatenate(rows, 0).T
        block = sums.shape[0] // count
        for entry in range(count):
            first = pl.multiple_of(places[entry] * block, 8)
            sums_low[entry * block : (entry + 1) * block, :] = sums[pl.ds(first, block), :]
        result = sums_low[...].astype(BF)
    else:
        result = given[0][...].astype(BF)
    keep[:, wide:] = result[:half]
    send[:, wide:] = result[half:]


def small_lists(places, left, rights, sums):
    count = places.shape[1]
    tokens, width = left.shape
    inside = width // count % 8 == 0
    given = [left if inside else lists_outside(places, left)] + list(rights)
    if sums and inside:
        given += list(sums)
    elif sums:
        table = jnp.pad(jnp.concatenate(sums, 0), ((0, LANES - len(sums)), (0, 0)))
        given.append(lists_outside(places, table)[0])
    wide = rights[0].shape[1] + (LANES if sums else 0)
    plain = (width, tokens) if inside else (8, LANES)
    beside = (width, LANES) if sums else (8, LANES)
    scratch = [
        pltpu.VMEM(plain, F32),
        pltpu.VMEM(plain, F32),
        pltpu.VMEM((1, width, tokens), BF),
        pltpu.VMEM(beside, F32),
        pltpu.VMEM(beside, F32),
    ]
    kernel = functools.partial(small_lists_kernel, count, inside, len(rights), bool(sums))
    scalars = jnp.concatenate([places[0], lax.axis_index("head").astype(jnp.int32).reshape(1)])
    return whole_call(kernel, [((width // 2, wide), BF)] * 2, scalars, *given, scratch=scratch)


def back_kernel(rest, feed, gate_s, up_s, gate_w, up_w, down_w, gate_out, up_out, rows_out, total):
    step = pl.program_id(0)
    last = pl.num_programs(0) - 1

    @pl.when(step == 0)
    def begin():
        total[...] = jnp.zeros_like(total)

    def tile(size):
        act_grad = dot_nt(feed[...], down_w[:size])
        gate_grad = (act_grad * gate_s[:, :size].astype(F32)).astype(BF)
        up_grad = (act_grad * up_s[:, :size].astype(F32)).astype(BF)
        gate_out[:, :size] = gate_grad
        up_out[:, :size] = up_grad
        total[...] += dot_nt(gate_grad, gate_w[:, :size]) + dot_nt(up_grad, up_w[:, :size])

    pl.when(step < last)(lambda: tile(gate_w.shape[1]))
    pl.when(step == last)(lambda: tile(rest))

    @pl.when(step == last)
    def finish():
        rows_out[...] = total[...].astype(BF)


def feed_back(feed, gate_s, up_s, gate_w, up_w, down_w):
    tokens, width = feed.shape
    hidden = gate_w.shape[1]
    tile = FEED_TILE
    steps, rest = steps_of(hidden, tile)
    return pl.pallas_call(
        functools.partial(back_kernel, rest),
        grid=(steps,),
        in_specs=[fixed((tokens, width))]
        + [columns(tokens, tile)] * 2
        + [columns(width, tile)] * 2
        + [pl.BlockSpec((tile, width), lambda i: (i, 0))],
        out_specs=[columns(tokens, tile)] * 2 + [fixed((tokens, width))],
        out_shape=[jax.ShapeDtypeStruct((tokens, hidden), BF)] * 2 + [jax.ShapeDtypeStruct((tokens, width), BF)],
        scratch_shapes=[pltpu.VMEM((tokens, width), F32)],
        cost_estimate=SMALL,
        compiler_params=pltpu.CompilerParams(vmem_limit_bytes=TILE_ROOM),
    )(feed, gate_s, up_s, gate_w, up_w, down_w)


def shards(
    hidden,
    positions,
    input_gain,
    query_weight,
    key_weight,
    value_weight,
    query_gain,
    key_gain,
    out_weight,
    branch_gain,
    middle_gain,
    gate_weight,
    up_weight,
    down_weight,
    final_gain,
    cotangent,
):
    packs, rows, width = hidden.shape
    size = key_weight.shape[1]
    heads = query_weight.shape[1] // size
    tokens = packs * rows
    groups = lax.axis_size(GROUPS)
    count = groups * packs
    head = lax.axis_index("head")
    place = lax.axis_index("quad")
    group = lax.axis_index(GROUPS)
    me = group * packs + place
    far_count = lax.axis_size("far")

    def places_of(*orders):
        return jnp.stack([list_places(order, packs, far_count) for order in orders])

    def as_row(gain):
        return gain.astype(F32).reshape(1, -1)

    gain_input, gain_query, gain_key = as_row(input_gain), as_row(query_gain), as_row(key_gain)
    gain_branch, gain_middle, gain_final = as_row(branch_gain), as_row(middle_gain), as_row(final_gain)

    pieces = to_packs(hidden, place)
    upstream_pieces = to_packs(cotangent, place)
    pack_position = lax.dynamic_slice(positions, (place, 0), (1, 1))[0, 0]
    start = (me * 2 + head) * rows - pack_position
    info = jnp.stack([group, place, head, start]).astype(jnp.int32)
    chips = group * packs + (jnp.arange(packs, dtype=jnp.int32) ^ place)
    firsts = (chips[None, :] * 2 + jnp.arange(2, dtype=jnp.int32)[:, None]) * rows
    token_index = firsts[:, :, None] + jnp.arange(rows, dtype=jnp.int32)
    angles = angles_for(token_index.reshape(2 * tokens) - start, size)
    cosine, sine = jnp.cos(angles), jnp.sin(angles)

    wide = heads * size
    own_tokens, key_raw, pair = whole_call(
        functools.partial(enter_kernel, packs),
        [((tokens, width), BF), ((tokens, size), F32), ((tokens, 2 * size), BF)],
        info,
        *pieces,
        gain_input,
        key_weight,
        value_weight,
        gain_key,
        cosine,
        sine,
    )
    other_tokens = over_head(own_tokens)
    pairs = [pair] + [shifted(pair, step) for step in range(1, groups)]
    tokens_both, normed_both, query_raw, queries = whole_call(
        functools.partial(query_kernel, heads),
        [((2 * tokens, width), BF), ((2 * tokens, width), BF), ((2 * tokens, wide), F32), ((2 * tokens, wide), BF)],
        info,
        own_tokens,
        other_tokens,
        gain_input,
        query_weight,
        gain_query,
        cosine,
        sine,
    )
    part = attend(info, queries, pairs, heads, packs)
    attended, totals, mixed, branch, residual, middle = whole_call(
        functools.partial(branch_kernel, heads),
        [
            ((2 * tokens, wide), F32),
            ((2 * tokens, LANES), F32),
            ((2 * tokens, wide), BF),
            ((2 * tokens, width), F32),
            ((2 * tokens, width), F32),
            ((2 * tokens, width), BF),
        ],
        info,
        part,
        over_head(part),
        tokens_both,
        out_weight,
        gain_branch,
        gain_middle,
    )
    middle, *upstream_pieces = tie(middle, *upstream_pieces)
    own_upstream = jnp.concatenate(upstream_pieces, 0)
    other_upstream = over_head(own_upstream)
    act, gate_s, up_s, feed_part = feed_forward(middle, gate_weight, up_weight, down_weight)
    output, upstream, feed_low, final_gain_sum = whole_call(
        finish_kernel,
        [((tokens, width), BF), ((2 * tokens, width), BF), ((2 * tokens, width), BF), ((1, width), F32)],
        info,
        feed_part,
        over_head(feed_part),
        residual,
        own_upstream,
        other_upstream,
        gain_final,
        scratch=[pltpu.VMEM((2 * tokens, width), F32)],
    )

    half_out = (width // 2 + LANES - 1) // LANES * LANES
    chains = {}
    ends = {}
    env = {}
    token = group

    def lists_of(first_name, left, right, cuts):
        nonlocal token
        names = range(first_name, first_name + len(cuts))
        orders = sorted({ORDERS[name] for name in names})
        route, at = [], 0
        for name, cut in zip(names, cuts):
            route.append((orders.index(ORDERS[name]), at, at + cut))
            at += cut
        found = weight_lists(places_of(*orders), left, right, tuple(route), LIST_TILE)
        token, *flat = tie(token, *sum([list(one) for one in found], []))
        for index, name in enumerate(names):
            steps = ORDERS[name][: STEPS[name]]
            chains[name] = Chain(flat[2 * index : 2 * index + 2], steps, len(steps) == 4)

    def compute_down():
        nonlocal token
        token, left, right = tie(token, feed_low, act)
        lists_of(DOWN, left, right, DOWN_CUTS)

    def compute_back():
        nonlocal token
        token, left = tie(token, feed_low)
        result = feed_back(left, gate_s, up_s, gate_weight, up_weight, down_weight)
        token, env["gate_low"], env["up_low"], env["middle_part"] = tie(token, *result)

    def compute_lists(name, source, cuts):
        nonlocal token
        token, left, right = tie(token, middle, env[source])
        lists_of(name, left, right, cuts)

    def compute_branch():
        nonlocal token
        result = whole_call(
            functools.partial(branch_back_kernel, heads),
            [
                ((2 * tokens, width), F32),
                ((2 * tokens, half_out), BF),
                ((2 * tokens, wide + LANES), BF),
                ((1, width), F32),
                ((1, width), F32),
            ],
            info,
            env["middle_part"],
            env[SEND_MIDDLE],
            residual,
            branch,
            upstream,
            attended,
            totals,
            out_weight,
            gain_middle,
            gain_branch,
        )
        token, *result = tie(token, *result)
        env["residual_grad"], env["branch_half"], env["scaled"], env["middle_gain"], env["branch_gain"] = result

    def compute_attention():
        nonlocal token
        token, scaled = tie(token, env["scaled"])
        token, env["query_part"], pair_part = tie(token, *attend_back(info, queries, scaled, pairs, heads, packs))
        ends[PAIRS] = summed_over(pair_part, GROUPS)

    def compute_out():
        nonlocal token
        token, left, right = tie(token, mixed, env["branch_half"])
        lists = small_lists(places_of(ORDERS[OUT]), left, (right,), ())
        token, *lists = tie(token, *lists)
        chains[OUT] = Chain(lists, ORDERS[OUT])

    def compute_query():
        nonlocal token
        result = whole_call(
            functools.partial(query_back_kernel, heads),
            [((2 * tokens, wide // 2), BF), ((1, size), F32), ((tokens, width), F32)],
            info,
            env["query_part"],
            env[SEND_GRAD],
            query_raw,
            gain_query,
            cosine,
            sine,
            query_weight,
            scratch=[pltpu.VMEM((2 * tokens, wide), BF)],
        )
        token, env["query_half"], env["query_gain"], env["back"] = tie(token, *result)

    def compute_query_lists():
        nonlocal token
        token, right = tie(token, env["query_half"])
        lists = small_lists(places_of(ORDERS[QUERY]), normed_both, (right,), ())
        token, *lists = tie(token, *lists)
        chains[QUERY] = Chain(lists, ORDERS[QUERY])

    def compute_key():
        nonlocal token
        result = whole_call(
            key_back_kernel,
            [((tokens, size), BF), ((tokens, size), BF), ((tokens, 2 * size), BF), ((1, size), F32)],
            info,
            ends[PAIRS],
            key_raw,
            gain_key,
            cosine,
            sine,
        )
        token, env["pair_mine"], env["pair_other"], env["pair_low"], env["key_gain"] = tie(token, *result)

    def compute_in():
        nonlocal token
        block = width // (2 * count)
        small = [env[name].reshape(count, 2, -1) for name in ("query_gain", "key_gain")]
        room = block - 2 * small[0].shape[2]
        small = jnp.concatenate(small + [jnp.zeros((count, 2, room), F32)], 2).reshape(1, width)
        sums = (env["branch_gain"], env["middle_gain"], final_gain_sum, small)
        token, mine = tie(token, env["pair_mine"])
        lists = small_lists(places_of(ORDERS[PAIR]), normed_both, (mine, env[SEND_PAIR]), sums)
        token, *lists = tie(token, *lists)
        chains[PAIR] = Chain(lists, ORDERS[PAIR])

    def compute_input():
        nonlocal token
        token, back = tie(token, env["back"])
        (rows_back,) = whole_call(
            leave_kernel,
            [((tokens, 2 * width), BF)],
            info,
            back,
            env["pair_low"],
            key_weight,
            value_weight,
            own_tokens,
            gain_input,
            env["residual_grad"],
            output,
        )
        token, rows_back = tie(token, rows_back)
        env["input_gradient"] = from_packs(rows_back, packs)

    def by_rows(reduced):
        rows_here = reduced.shape[0] // 2
        mine = lax.dynamic_slice_in_dim(reduced, head * rows_here, rows_here, 0)
        other = over_head(lax.dynamic_slice_in_dim(reduced, (1 - head) * rows_here, rows_here, 0))
        return mine, other

    works = {
        DOWN: compute_down,
        BACK: compute_back,
        GATE: lambda: compute_lists(GATE, "gate_low", GATE_CUTS),
        UP: lambda: compute_lists(UP, "up_low", UP_CUTS),
        BRANCH: compute_branch,
        ATTEND: compute_attention,
        OUT: compute_out,
        QUERY: compute_query,
        QUERY_LISTS: compute_query_lists,
        PAIR: compute_key,
        PAIR_LISTS: compute_in,
        INPUT: compute_input,
    }
    sends = {SEND_MIDDLE: "middle_part", SEND_GRAD: "query_part", SEND_PAIR: "pair_other"}
    flights = {}
    for kind, name in PLAN:
        if kind == WORK:
            works[name]()
        elif kind == SEND:
            token, value = tie(token, env[sends[name]])
            flights[name] = over_head(value)
        elif kind == TAKE and name == INPUT:
            token, *env["input_gradient"] = tie(token, *env["input_gradient"])
        elif kind == TAKE:
            token, env[name] = tie(token, flights[name])
        elif kind == START:
            token = chains[name].start(token)
        elif kind == LAND:
            token = chains[name].land(token)
            if chains[name].rest is None:
                continue
            if name in (OUT, QUERY, PAIR):
                ends[name] = summed_over(chains[name].rest, GROUPS)
            for joint, (sources, steps) in JOINTS.items():
                if joint in chains or joint in ends or any(s not in chains or chains[s].rest is None for s in sources):
                    continue
                total = jnp.concatenate([chains[source].rest for source in sources], 1)
                if steps:
                    token, *lists = tie(token, *halves(total))
                    chains[joint] = Chain(lists, steps, steps[-1] == FAR)
                else:
                    token, total = tie(token, total)
                    ends[joint] = summed_over(total, GROUPS)
        else:
            token, ends[name] = tie(token, ends[name])

    def result(*names):
        return jnp.concatenate([ends[n].astype(F32) if n in ends else chains[n].rest for n in names], 1)

    down_sum, gate_sum, up_sum = result(*DOWN_RESULT), result(*GATE_RESULT), result(*UP_RESULT)
    lower = head == 0

    def in_order(mine, other):
        return jnp.where(lower, mine, other).astype(F32), jnp.where(lower, other, mine).astype(F32)

    first, second = in_order(*by_rows(ends[OUT]))
    out_sum = jnp.concatenate([first, second[:, 2 * half_out - width :]], 1)
    query_sum = jnp.concatenate(in_order(*by_rows(ends[QUERY])), 1)
    mine, other = by_rows(ends[PAIR])
    key_sum, value_sum = in_order(mine[:, :size], other[:, :size])
    sums = mine[:, size:].astype(F32) + other[:, size:].astype(F32)
    in_sum = jnp.concatenate([query_sum, key_sum, value_sum], 1)
    first_row = (2 * me + head) * in_sum.shape[0]
    token_row = (2 * (token * packs + place) + head) * in_sum.shape[0]
    weight = jnp.concatenate(
        [
            lax.dynamic_slice_in_dim(one, first_row, in_sum.shape[0], 0)
            for one in (query_weight, key_weight, value_weight)
        ],
        1,
    )
    gain_piece = lax.dynamic_slice_in_dim(gain_input[0], token_row, in_sum.shape[0], 0)
    input_gain_sum = jnp.sum(weight.astype(F32) * in_sum, 1) / gain_piece
    few = size // (2 * count)

    rows_back = in_place(env["input_gradient"], place)

    return (
        rows_back[:, :, width:],
        rows_back[:, :, :width].astype(F32),
        input_gain_sum,
        query_sum,
        key_sum,
        value_sum,
        sums[:few, 3],
        sums[few : 2 * few, 3],
        out_sum,
        sums[:, 0],
        sums[:, 1],
        gate_sum,
        up_sum,
        down_sum.T,
        sums[:, 2],
    )


def solution(mesh):
    packs = 4
    split = Mesh(
        mesh.devices.reshape(-1, 2, packs, mesh.shape["head"]), ("far", "near", "quad", "head")
    )
    seq_axes = ("far", "near", "quad")
    all_axes = seq_axes + ("head",)
    tokens = P(None, all_axes, None)
    both = P(all_axes)
    both_rows = P(all_axes, None)
    in_specs = (
        tokens,
        P(None, all_axes),
        P(),
        P(),
        P(),
        P(),
        P(),
        P(),
        P(),
        P(),
        P(),
        P(None, "head"),
        P(None, "head"),
        P("head", None),
        P(),
        tokens,
    )
    out_specs = (
        tokens,
        tokens,
        both,
        both_rows,
        both_rows,
        both_rows,
        both,
        both,
        both_rows,
        both,
        both,
        P(seq_axes, "head"),
        P(seq_axes, "head"),
        P("head", seq_axes),
        both,
    )
    return jax.shard_map(shards, mesh=split, in_specs=in_specs, out_specs=out_specs, check_vma=False)
```

```python
import functools
import math

import jax
import jax.numpy as jnp
from jax import lax
from jax.experimental import pallas as pl
from jax.experimental.pallas import tpu as pltpu
from jax.sharding import Mesh, PartitionSpec as P

EPS = 1e-06
BASE = 1000000.0
BF = jnp.bfloat16
F32 = jnp.float32
LANES = 128
MEGA = 1024 * 1024
FEED_TILE, LIST_TILE = 512, 1024
VMEM = 56 * MEGA
WHOLE_ROOM, TILE_ROOM = 56 * MEGA, 56 * MEGA
SMALL = pl.CostEstimate(flops=1, bytes_accessed=1, transcendentals=0)


def normed(values, gain):
    return values * lax.rsqrt(jnp.mean(values * values, -1, keepdims=True) + EPS) * gain


def normed_back(values, gain, grad):
    scale = lax.rsqrt(jnp.mean(values * values, -1, keepdims=True) + EPS)
    pull = grad * gain
    shared = jnp.mean(values * pull, -1, keepdims=True) * (scale * scale * scale)
    return scale * pull - values * shared, jnp.sum(grad * values * scale, 0, keepdims=True)


def turned(values, cosine, sine, way):
    half = values.shape[-1] // 2
    first, second = values[:, :half], values[:, half:]
    return jnp.concatenate([first * cosine - way * second * sine, second * cosine + way * first * sine], -1)


def angles_for(positions, head_size):
    half_size = head_size // 2
    frequency = jnp.exp(
        jnp.arange(half_size, dtype=jnp.float32) * (-2.0 * math.log(BASE) / head_size)
    )
    return positions.astype(jnp.float32)[..., None] * frequency


def dot(left, right):
    return jnp.dot(left, right, preferred_element_type=F32)


def dot_nt(left, right):
    return lax.dot_general(left, right, (((1,), (1,)), ((), ())), preferred_element_type=F32)


def dot_tn(left, right):
    return lax.dot_general(left, right, (((0,), (0,)), ((), ())), preferred_element_type=F32)


def bits_of(count):
    return count.bit_length() - 1


DOWN, GATE, UP = 0, 10, 20
OUT, QUERY, PAIR, PAIRS = range(30, 34)
BACK, BRANCH, ATTEND, QUERY_LISTS, PAIR_LISTS, INPUT = range(40, 46)
SEND_MIDDLE, SEND_GRAD, SEND_PAIR = range(50, 53)
JOINT = 60
ALONG_X, ALONG_Y, NEAR, FAR = range(4)
DOWN_CUTS = (2, 2)
GATE_CUTS = (2, 2)
UP_CUTS = (1, 1, 2)
ORDERS = {
    DOWN: (ALONG_X, ALONG_Y),
    DOWN + 1: (ALONG_Y, ALONG_X),
    GATE: (ALONG_Y, ALONG_X, NEAR, FAR),
    GATE + 1: (ALONG_X, ALONG_Y, NEAR, FAR),
    UP: (ALONG_X, ALONG_Y, NEAR, FAR),
    UP + 1: (ALONG_Y, ALONG_X, NEAR, FAR),
    UP + 2: (NEAR, ALONG_X, ALONG_Y, FAR),
    OUT: (ALONG_X, ALONG_Y),
    QUERY: (ALONG_Y, ALONG_X),
    PAIR: (ALONG_Y, ALONG_X),
}
STEPS = {DOWN: 2, DOWN + 1: 2, GATE: 2, GATE + 1: 2, UP: 2, UP + 1: 2, UP + 2: 4, OUT: 2, QUERY: 2, PAIR: 2}
JOINTS = {
    JOINT: ((DOWN, DOWN + 1), ()),
    JOINT + 1: ((GATE, GATE + 1), (NEAR, FAR)),
    JOINT + 2: ((UP, UP + 1), (NEAR, FAR)),
}
DOWN_RESULT = (JOINT,)
GATE_RESULT = (JOINT + 1,)
UP_RESULT = (JOINT + 2, UP + 2)
WORK, SEND, TAKE, START, LAND, END = range(6)
PLAN = (
    (WORK, DOWN),
    (START, DOWN + 1),
    (START, DOWN),
    (WORK, BACK),
    (SEND, SEND_MIDDLE),
    (WORK, GATE),
    (START, GATE + 1),
    (START, GATE),
    (WORK, UP),
    (TAKE, SEND_MIDDLE),
    (WORK, BRANCH),
    (START, UP + 2),
    (LAND, DOWN + 1),
    (LAND, DOWN),
    (START, DOWN),
    (WORK, OUT),
    (WORK, ATTEND),
    (START, DOWN + 1),
    (START, OUT),
    (LAND, GATE + 1),
    (LAND, GATE),
    (START, UP + 1),
    (START, GATE + 1),
    (SEND, SEND_GRAD),
    (START, UP),
    (LAND, DOWN + 1),
    (START, GATE),
    (LAND, DOWN),
    (END, PAIRS),
    (LAND, OUT),
    (TAKE, SEND_GRAD),
    (WORK, PAIR),
    (SEND, SEND_PAIR),
    (WORK, QUERY),
    (LAND, UP + 2),
    (LAND, UP + 1),
    (LAND, GATE),
    (WORK, QUERY_LISTS),
    (TAKE, SEND_PAIR),
    (START, QUERY),
    (START, UP + 2),
    (START, OUT),
    (LAND, GATE + 1),
    (WORK, PAIR_LISTS),
    (START, PAIR),
    (START, JOINT + 1),
    (LAND, QUERY),
    (LAND, UP),
    (START, UP),
    (LAND, OUT),
    (LAND, PAIR),
    (START, UP + 1),
    (LAND, UP + 2),
    (END, JOINT),
    (START, PAIR),
    (START, UP + 2),
    (LAND, JOINT + 1),
    (START, JOINT + 1),
    (LAND, PAIR),
    (START, QUERY),
    (LAND, UP),
    (LAND, UP + 2),
    (WORK, INPUT),
    (LAND, UP + 1),
    (START, JOINT + 2),
    (START, UP + 2),
    (LAND, JOINT + 1),
    (LAND, QUERY),
    (LAND, JOINT + 2),
    (START, JOINT + 2),
    (END, OUT),
    (LAND, UP + 2),
    (LAND, JOINT + 2),
    (TAKE, INPUT),
    (END, PAIR),
    (END, QUERY),
)

GROUPS = ("far", "near")


def exchanged(value, mask, axis="quad"):
    count = lax.axis_size(axis)
    return lax.ppermute(value, axis, [(i, i ^ mask) for i in range(count)])


def shifted(value, step):
    count = lax.axis_size(GROUPS)
    return lax.ppermute(value, GROUPS, [(i, i + step) for i in range(count) if 0 <= i + step < count])


def over_head(value):
    return lax.ppermute(value, "head", [(0, 1), (1, 0)])


def over_step(value, step):
    if step in (NEAR, FAR):
        return exchanged(value, 1, GROUPS[1] if step == NEAR else GROUPS[0])
    return exchanged(value, 1 << step)


def to_packs(value, place):
    pieces = [lax.dynamic_index_in_dim(value, place, 0, False)]
    for mask in range(1, value.shape[0]):
        pieces.append(exchanged(lax.dynamic_index_in_dim(value, place ^ mask, 0, False), mask))
    return pieces


def from_packs(value, packs):
    rows = value.shape[0] // packs
    pieces = [value[mask * rows : (mask + 1) * rows] for mask in range(packs)]
    return [pieces[0]] + [exchanged(pieces[mask], mask) for mask in range(1, packs)]


def in_place(pieces, place):
    blocks = jnp.stack(pieces).reshape((2, 2) + pieces[0].shape)
    blocks = jnp.where(place & 1 == 1, jnp.flip(blocks, 1), blocks)
    blocks = jnp.where(place & 2 == 2, jnp.flip(blocks, 0), blocks)
    return blocks.reshape((len(pieces),) + pieces[0].shape)


def tie(token, *values):
    result = lax.optimization_barrier((token,) + values)
    return result


def list_places(order, packs, far_count):
    sizes = {ALONG_X: 2, ALONG_Y: 2, NEAR: 2, FAR: far_count}
    own = {NEAR: lax.axis_index("near"), FAR: lax.axis_index("far")}
    own[ALONG_X], own[ALONG_Y] = lax.axis_index("quad") & 1, lax.axis_index("quad") >> 1
    rest = jnp.arange(2 * packs * far_count, dtype=jnp.int32)
    at = {}
    for step in reversed(tuple(order) + tuple(step for step in (FAR, NEAR) if step not in order)):
        digit = rest % sizes[step]
        at[step] = digit ^ own[step] if step in order and sizes[step] == 2 else digit
        rest = rest // sizes[step]
    return ((at[FAR] * 2 + at[NEAR]) * packs + at[ALONG_Y] * 2 + at[ALONG_X]).astype(jnp.int32)


class Chain:
    def __init__(self, lists, order, last=False):
        self.keep, self.send = lists
        self.order = order
        self.last = last
        self.stage = 0
        self.rest = None

    def whole(self):
        return self.order[self.stage] == FAR and lax.axis_size("far") > 2

    def start(self, token):
        if not self.whole():
            token, send = tie(token, self.send)
            self.flight = over_step(send, self.order[self.stage])
        return token

    def land(self, token):
        if self.whole():
            total = summed_over(jnp.concatenate([self.keep, self.send], 0), "far")
            self.stage += 1
            if self.stage == len(self.order):
                self.rest = total.astype(F32)
            else:
                self.keep, self.send = halves(total)
            return token
        token, arrived, keep = tie(token, self.flight, self.keep)
        self.stage += 1
        if self.stage == len(self.order):
            total = keep.astype(F32) + arrived.astype(F32)
            token, self.rest = tie(token, total if self.last else total.astype(BF))
            return token
        half = keep.shape[0] // 2
        send = (keep[half:].astype(F32) + arrived[half:].astype(F32)).astype(BF)
        keep = (keep[:half].astype(F32) + arrived[:half].astype(F32)).astype(BF)
        token, self.keep, self.send = tie(token, keep, send)
        return token


def halves(total):
    half = total.shape[0] // 2
    return total[:half], total[half:]


def summed_over(value, axes):
    return lax.psum_scatter(value, axes, scatter_dimension=0, tiled=True)


def allowed_mask(info, rows, packs, length):
    group, place, head, start = info[0], info[1], info[2], info[3]
    span = rows * packs
    column = lax.broadcasted_iota(jnp.int32, (1, length), 1)
    chip = (group - column // span) * packs + ((column % span) // rows ^ place)
    key_index = (chip * 2 + head) * rows + column % rows
    row = lax.broadcasted_iota(jnp.int32, (2 * span, 1), 0)
    chip = group * packs + ((row % span) // rows ^ place)
    query_index = (chip * 2 + row // span) * rows + row % rows
    return (key_index >= start) & (key_index <= query_index)


def attend_kernel(heads, rows, packs, groups, info, queries, *refs):
    pairs, (out,) = refs[:groups], refs[groups:]
    size = queries.shape[1] // heads
    keys = jnp.concatenate([ref[:, :size] for ref in pairs], 0)
    values = jnp.concatenate([ref[:, size:] for ref in pairs], 0)
    allowed = allowed_mask(info, rows, packs, keys.shape[0])
    lane = lax.broadcasted_iota(jnp.int32, (queries.shape[0], LANES), 1)
    lanes = jnp.zeros(lane.shape, F32)
    for h in range(heads):
        cut = slice(h * size, (h + 1) * size)
        expo = jnp.where(allowed, jnp.exp(dot_nt(queries[:, cut], keys)), 0.0)
        totals = jnp.sum(expo, -1, keepdims=True)
        out[:, cut] = dot(expo.astype(BF), values).astype(BF)
        high = totals.astype(BF).astype(F32)
        lanes = jnp.where(lane == h, high, jnp.where(lane == heads + h, totals - high, lanes))
    out[:, heads * size :] = lanes.astype(BF)


def attend_back_kernel(heads, rows, packs, groups, info, queries, grads, *refs):
    pairs, (query_out, pair_out) = refs[:groups], refs[groups:]
    span = rows * packs
    size = queries.shape[1] // heads
    keys = jnp.concatenate([ref[:, :size] for ref in pairs], 0)
    values = jnp.concatenate([ref[:, size:] for ref in pairs], 0)
    allowed = allowed_mask(info, rows, packs, keys.shape[0])
    key_grad = jnp.zeros(keys.shape, F32)
    value_grad = jnp.zeros(keys.shape, F32)
    lanes = grads[:, heads * size :].astype(F32)
    for h in range(heads):
        cut = slice(h * size, (h + 1) * size)
        query, grad = queries[:, cut], grads[:, cut]
        delta = lanes[:, h : h + 1] + lanes[:, heads + h : heads + h + 1]
        expo = jnp.where(allowed, jnp.exp(dot_nt(query, keys)), 0.0)
        score_grad = (expo * (dot_nt(grad, values) - delta)).astype(BF)
        query_out[:, cut] = (dot(score_grad, keys) * (size**-0.5)).astype(BF)
        key_grad = key_grad + dot_tn(score_grad, query)
        value_grad = value_grad + dot_tn(expo.astype(BF), grad)
    both = jnp.concatenate([key_grad, value_grad], 1).astype(BF)
    for index in range(groups):
        target = lax.rem(info[0] - index + groups, groups) * span
        pair_out[pl.ds(pl.multiple_of(target, span), span), :] = both[index * span : (index + 1) * span]


def room(args, outs, scratch):
    sizes = [math.prod(one.shape) * one.dtype.itemsize for one in args]
    sizes += [math.prod(shape) * jnp.dtype(kind).itemsize for shape, kind in outs]
    sizes += [math.prod(one.shape) * jnp.dtype(one.dtype).itemsize for one in scratch]
    return min(VMEM, sum(sizes) + max(sum(sizes), WHOLE_ROOM))


def whole_call(kernel, outs, *args, scratch=()):
    spec = pl.BlockSpec(memory_space=pltpu.VMEM)
    return pl.pallas_call(
        kernel,
        in_specs=[pl.BlockSpec(memory_space=pltpu.SMEM)] + [spec] * (len(args) - 1),
        out_specs=[spec] * len(outs),
        out_shape=[jax.ShapeDtypeStruct(*out) for out in outs],
        scratch_shapes=list(scratch),
        cost_estimate=SMALL,
        compiler_params=pltpu.CompilerParams(vmem_limit_bytes=room(args[1:], outs, scratch)),
    )(*args)


def attend(info, queries, pairs, heads, packs):
    tokens, width = queries.shape
    kernel = functools.partial(attend_kernel, heads, tokens // 2 // packs, packs, len(pairs))
    return whole_call(kernel, [((tokens, width + LANES), BF)], info, queries, *pairs)[0]


def attend_back(info, queries, grads, pairs, heads, packs):
    tokens, width = queries.shape
    outs = [((tokens, width), BF), ((len(pairs) * tokens // 2, pairs[0].shape[1]), BF)]
    kernel = functools.partial(attend_back_kernel, heads, tokens // 2 // packs, packs, len(pairs))
    return whole_call(kernel, outs, info, queries, grads, *pairs)


def own_rows(info, ref):
    span = ref.shape[0] // 2
    return ref[pl.ds(pl.multiple_of(info[2] * span, span), span), :]


def by_core(info, own, other):
    lower = info[2] == 0
    return jnp.concatenate([jnp.where(lower, own, other), jnp.where(lower, other, own)], 0)


def sum_of(part, arrived):
    return part[...].astype(F32) + arrived[...].astype(F32)


def enter_kernel(count, info, *refs):
    pieces = refs[:count]
    gain, key_w, value_w, key_gain, cosine, sine, tokens_out, raw_out, pair_out = refs[count:]
    tokens = jnp.concatenate([piece[...] for piece in pieces], 0)
    tokens_out[...] = tokens
    rows = normed(tokens.astype(F32), gain[...]).astype(BF)
    raw = dot(rows, key_w[...])
    raw_out[...] = raw
    size = raw.shape[1]
    turn = turned(normed(raw, key_gain[...]), own_rows(info, cosine), own_rows(info, sine), 1.0)
    pair_out[:, :size] = turn.astype(BF)
    pair_out[:, size:] = dot(rows, value_w[...]).astype(BF)


def query_kernel(heads, info, own, other, gain, query_w, query_gain, cosine, sine, *outs):
    tokens_out, normed_out, raw_out, query_out = outs
    tokens = by_core(info, own[...], other[...])
    tokens_out[...] = tokens
    rows = normed(tokens.astype(F32), gain[...]).astype(BF)
    normed_out[...] = rows
    raw = dot(rows, query_w[...])
    raw_out[...] = raw
    size = raw.shape[1] // heads
    for h in range(heads):
        cut = slice(h * size, (h + 1) * size)
        turn = turned(normed(raw[:, cut], query_gain[...]), cosine[...], sine[...], 1.0).astype(BF)
        query_out[:, cut] = (turn.astype(F32) * (size**-0.5)).astype(BF)


def branch_kernel(heads, info, part, arrived, tokens, out_w, branch_gain, middle_gain, *outs):
    attended_out, total_out, mixed_out, branch_out, residual_out, middle_out = outs
    width = attended_out.shape[1]
    size = width // heads
    lanes = sum_of(part.at[:, width:], arrived.at[:, width:])
    lane = lax.broadcasted_iota(jnp.int32, lanes.shape, 1)
    totals = jnp.zeros(lanes.shape, F32)
    for h in range(heads):
        cut = slice(h * size, (h + 1) * size)
        total = lanes[:, h : h + 1] + lanes[:, heads + h : heads + h + 1]
        attended = sum_of(part.at[:, cut], arrived.at[:, cut]) / total
        attended_out[:, cut] = attended
        mixed_out[:, cut] = attended.astype(BF)
        totals = jnp.where(lane == h, total, totals)
    total_out[...] = totals
    branch = dot(mixed_out[...], out_w[...])
    branch_out[...] = branch
    residual = tokens[...].astype(F32) + normed(branch, branch_gain[...])
    residual_out[...] = residual
    middle_out[...] = normed(residual, middle_gain[...]).astype(BF)


def finish_kernel(info, part, arrived, residual, own, other, gain, output, upstream_out, grad_out, gain_out, rows):
    upstream = by_core(info, own[...], other[...])
    upstream_out[...] = upstream
    feed = sum_of(part, arrived)
    rows[...] = residual[...] + normed(feed, gain[...])
    output[...] = own_rows(info, rows).astype(BF)
    grad, gain_grad = normed_back(feed, gain[...], upstream.astype(F32))
    grad_out[...] = grad.astype(BF)
    gain_out[...] = 0.5 * gain_grad


def branch_back_kernel(heads, info, part, arrived, residual, branch, upstream, attended, totals, out_w, *refs):
    middle_gain, branch_gain, grad_out, half_out, scaled_out, middle_sum, branch_sum = refs
    part, gain_grad = normed_back(residual[...], middle_gain[...], sum_of(part, arrived))
    middle_sum[...] = 0.5 * gain_grad
    residual_grad = upstream[...].astype(F32) + part
    grad_out[...] = residual_grad
    branch_grad, gain_grad = normed_back(branch[...], branch_gain[...], residual_grad)
    branch_sum[...] = 0.5 * gain_grad
    low = branch_grad.astype(BF)
    half = half_out.shape[1]
    half_out[...] = jnp.where(info[2] == 0, low[:, :half], low[:, low.shape[1] - half :])
    mixed_grad = dot_nt(low, out_w[...]).astype(BF).astype(F32)
    width = mixed_grad.shape[1]
    size = width // heads
    lane = lax.broadcasted_iota(jnp.int32, (low.shape[0], LANES), 1)
    lanes = jnp.zeros(lane.shape, F32)
    for h in range(heads):
        cut = slice(h * size, (h + 1) * size)
        total = totals[:, h : h + 1]
        scaled_out[:, cut] = (mixed_grad[:, cut] / total).astype(BF)
        delta = jnp.sum(mixed_grad[:, cut] * attended[:, cut], -1, keepdims=True) / total
        high = delta.astype(BF).astype(F32)
        lanes = jnp.where(lane == h, high, jnp.where(lane == heads + h, delta - high, lanes))
    scaled_out[:, width:] = lanes.astype(BF)


def query_back_kernel(heads, info, part, arrived, raw, gain, cosine, sine, query_w, half_out, sum_out, back_out, low):
    size = raw.shape[1] // heads
    gain_sum = jnp.zeros((1, size), F32)
    for h in range(heads):
        cut = slice(h * size, (h + 1) * size)
        grad = sum_of(part.at[:, cut], arrived.at[:, cut]).astype(BF).astype(F32)
        grad, more = normed_back(raw[:, cut], gain[...], turned(grad, cosine[...], sine[...], -1.0))
        low[:, cut] = grad.astype(BF)
        gain_sum = gain_sum + more
    sum_out[...] = 0.5 * gain_sum
    half = half_out.shape[1]
    half_out[...] = jnp.where(info[2] == 0, low[:, :half], low[:, half:])
    back_out[...] = dot_nt(own_rows(info, low), query_w[...])


def key_back_kernel(info, pair_grad, raw, gain, cosine, sine, mine_out, other_out, low_out, sum_out):
    size = raw.shape[1]
    turned_grad = turned(pair_grad[:, :size].astype(F32), own_rows(info, cosine), own_rows(info, sine), -1.0)
    grad, sum_out[...] = normed_back(raw[...], gain[...], turned_grad)
    low, value = grad.astype(BF), pair_grad[:, size:]
    low_out[:, :size] = low
    low_out[:, size:] = value
    lower = info[2] == 0
    mine_out[...] = jnp.where(lower, low, value)
    other_out[...] = jnp.where(lower, value, low)


def leave_kernel(info, back, low, key_w, value_w, tokens, gain, residual_grad, output, rows_out):
    size, width = key_w.shape[1], tokens.shape[1]
    rows_out[:, width:] = output[...]
    grad = back[...] + dot_nt(low[:, :size], key_w[...]) + dot_nt(low[:, size:], value_w[...])
    part, ignored = normed_back(tokens[...].astype(F32), gain[...], grad)
    rows_out[:, :width] = (own_rows(info, residual_grad) + part).astype(BF)


def feed_kernel(rest, rows, gate_w, up_w, down_w, act_out, gate_out, up_out, feed_out, total):
    step = pl.program_id(0)
    last = pl.num_programs(0) - 1

    @pl.when(step == 0)
    def begin():
        total[...] = jnp.zeros_like(total)

    def tile(size):
        gate = dot(rows[...], gate_w[:, :size])
        upward = dot(rows[...], up_w[:, :size])
        root = math.sqrt(2.0 / math.pi)
        square = gate * gate
        bend = jnp.tanh(gate * (root + (root * 0.044715) * square))
        half = 0.5 + 0.5 * bend
        gelu = gate * half
        slope = half + (0.5 * gate) * (1.0 - bend * bend) * (root + (3 * 0.044715 * root) * square)
        act = (gelu * upward).astype(BF)
        act_out[:, :size] = act
        gate_out[:, :size] = (slope * upward).astype(BF)
        up_out[:, :size] = gelu.astype(BF)
        total[...] += dot(act, down_w[:size])

    pl.when(step < last)(lambda: tile(gate_w.shape[1]))
    pl.when(step == last)(lambda: tile(rest))

    @pl.when(step == last)
    def finish():
        feed_out[...] = total[...].astype(BF)


def steps_of(length, tile):
    steps = -(-length // tile)
    return steps, length - (steps - 1) * tile


def fixed(shape):
    return pl.BlockSpec(shape, lambda i, *_: (0,) * len(shape))


def columns(rows, tile):
    return pl.BlockSpec((rows, tile), lambda i, *_: (0, i))


def feed_forward(rows, gate_w, up_w, down_w):
    tokens, width = rows.shape
    hidden = gate_w.shape[1]
    tile = FEED_TILE
    steps, rest = steps_of(hidden, tile)
    return pl.pallas_call(
        functools.partial(feed_kernel, rest),
        grid=(steps,),
        in_specs=[
            fixed((tokens, width)),
            columns(width, tile),
            columns(width, tile),
            pl.BlockSpec((tile, width), lambda i: (i, 0)),
        ],
        out_specs=[columns(tokens, tile)] * 3 + [fixed((tokens, width))],
        out_shape=[jax.ShapeDtypeStruct((tokens, hidden), BF)] * 3 + [jax.ShapeDtypeStruct((tokens, width), BF)],
        scratch_shapes=[pltpu.VMEM((tokens, width), F32)],
        cost_estimate=SMALL,
        compiler_params=pltpu.CompilerParams(vmem_limit_bytes=TILE_ROOM),
    )(rows, gate_w, up_w, down_w)


def put_lists(left, plain, listed, low, places, count, orders):
    plain[...] = left[...].astype(F32).T
    block = plain.shape[0] // count
    for which in range(orders):
        for entry in range(count):
            first = places[which * count + entry] * block
            if block % 8 == 0:
                first = pl.multiple_of(first, 8)
            listed[entry * block : (entry + 1) * block, :] = plain[pl.ds(first, block), :]
        low[which] = listed[...].astype(BF)


def lists_outside(places, left):
    blocks = left.T.reshape(places.shape[1], -1, left.shape[0])
    return jnp.stack([jnp.take(blocks, place, axis=0).reshape(left.shape[1], -1) for place in places])


def emit(result, outs):
    if len(outs) == 1:
        outs[0][...] = result
    else:
        half = result.shape[0] // 2
        outs[0][...] = result[:half]
        outs[1][...] = result[half:]


def span_spec(rows, tile, first, last):
    return pl.BlockSpec((rows, tile), lambda i, *_: (0, jnp.clip(i - first, 0, last - first - 1)))


def wgrad_kernel(count, orders, route, cuts, inside, places, left, right, *refs):
    step = pl.program_id(0)
    outs, (plain, listed, low) = refs[:-3], refs[-3:]

    @pl.when(step == 0)
    def begin():
        if inside:
            put_lists(left, plain, listed, low, places, count, orders)
        else:
            low[...] = left[...]

    for index, (order, first, last) in enumerate(route):

        @pl.when((step >= first) & (step < last))
        def piece(index=index, order=order):
            emit(dot(low[order], right[...]).astype(BF), outs[cuts[index][0] : cuts[index][1]])


def weight_lists(places, left, right, route, tile):
    tokens, width = left.shape
    orders, count = places.shape
    steps, ignored = steps_of(right.shape[1], tile)
    outs, specs, cuts = [], [], []
    for ignored, first, last in route:
        cuts.append((len(outs), len(outs) + 2))
        for ignored in range(2):
            outs.append(jax.ShapeDtypeStruct((width // 2, min(last * tile, right.shape[1]) - first * tile), BF))
            specs.append(span_spec(width // 2, tile, first, last))
    inside = width // count % 8 == 0
    given = left if inside else lists_outside(places, left)
    plain = (width, tokens) if inside else (8, LANES)
    result = pl.pallas_call(
        functools.partial(wgrad_kernel, count, orders, route, cuts, inside),
        grid_spec=pltpu.PrefetchScalarGridSpec(
            num_scalar_prefetch=1,
            grid=(steps,),
            in_specs=[fixed(given.shape), columns(tokens, tile)],
            out_specs=specs,
            scratch_shapes=[
                pltpu.VMEM(plain, F32),
                pltpu.VMEM(plain, F32),
                pltpu.VMEM((orders, width, tokens), BF),
            ],
        ),
        out_shape=outs,
        cost_estimate=SMALL,
        compiler_params=pltpu.CompilerParams(vmem_limit_bytes=TILE_ROOM),
    )(places.reshape(-1), given, right)
    return [result[first:last] for first, last in cuts]


def small_lists_kernel(count, inside, rights, with_sums, places, left, *refs):
    right = refs[0][...]
    if rights == 2:
        lower = places[count] == 0
        other = refs[1][...]
        right = jnp.concatenate([jnp.where(lower, right, other), jnp.where(lower, other, right)], 0)
    refs = refs[rights:]
    given, (keep, send), (plain, listed, low, sums, sums_low) = refs[:-7], refs[-7:-5], refs[-5:]
    if inside:
        put_lists(left, plain, listed, low, places, count, 1)
    else:
        low[...] = left[...]
    wide = right.shape[1]
    half = low.shape[1] // 2
    result = dot(low[0], right).astype(BF)
    keep[:, :wide] = result[:half]
    send[:, :wide] = result[half:]
    if not with_sums:
        return
    if inside:
        rows = [one[...] for one in given]
        rows.append(jnp.zeros((LANES - len(rows), rows[0].shape[1]), F32))
        sums[...] = jnp.concatenate(rows, 0).T
        block = sums.shape[0] // count
        for entry in range(count):
            first = pl.multiple_of(places[entry] * block, 8)
            sums_low[entry * block : (entry + 1) * block, :] = sums[pl.ds(first, block), :]
        result = sums_low[...].astype(BF)
    else:
        result = given[0][...].astype(BF)
    keep[:, wide:] = result[:half]
    send[:, wide:] = result[half:]


def small_lists(places, left, rights, sums):
    count = places.shape[1]
    tokens, width = left.shape
    inside = width // count % 8 == 0
    given = [left if inside else lists_outside(places, left)] + list(rights)
    if sums and inside:
        given += list(sums)
    elif sums:
        table = jnp.pad(jnp.concatenate(sums, 0), ((0, LANES - len(sums)), (0, 0)))
        given.append(lists_outside(places, table)[0])
    wide = rights[0].shape[1] + (LANES if sums else 0)
    plain = (width, tokens) if inside else (8, LANES)
    beside = (width, LANES) if sums else (8, LANES)
    scratch = [
        pltpu.VMEM(plain, F32),
        pltpu.VMEM(plain, F32),
        pltpu.VMEM((1, width, tokens), BF),
        pltpu.VMEM(beside, F32),
        pltpu.VMEM(beside, F32),
    ]
    kernel = functools.partial(small_lists_kernel, count, inside, len(rights), bool(sums))
    scalars = jnp.concatenate([places[0], lax.axis_index("head").astype(jnp.int32).reshape(1)])
    return whole_call(kernel, [((width // 2, wide), BF)] * 2, scalars, *given, scratch=scratch)


def back_kernel(rest, feed, gate_s, up_s, gate_w, up_w, down_w, gate_out, up_out, rows_out, total):
    step = pl.program_id(0)
    last = pl.num_programs(0) - 1

    @pl.when(step == 0)
    def begin():
        total[...] = jnp.zeros_like(total)

    def tile(size):
        act_grad = dot_nt(feed[...], down_w[:size])
        gate_grad = (act_grad * gate_s[:, :size].astype(F32)).astype(BF)
        up_grad = (act_grad * up_s[:, :size].astype(F32)).astype(BF)
        gate_out[:, :size] = gate_grad
        up_out[:, :size] = up_grad
        total[...] += dot_nt(gate_grad, gate_w[:, :size]) + dot_nt(up_grad, up_w[:, :size])

    pl.when(step < last)(lambda: tile(gate_w.shape[1]))
    pl.when(step == last)(lambda: tile(rest))

    @pl.when(step == last)
    def finish():
        rows_out[...] = total[...].astype(BF)


def feed_back(feed, gate_s, up_s, gate_w, up_w, down_w):
    tokens, width = feed.shape
    hidden = gate_w.shape[1]
    tile = FEED_TILE
    steps, rest = steps_of(hidden, tile)
    return pl.pallas_call(
        functools.partial(back_kernel, rest),
        grid=(steps,),
        in_specs=[fixed((tokens, width))]
        + [columns(tokens, tile)] * 2
        + [columns(width, tile)] * 2
        + [pl.BlockSpec((tile, width), lambda i: (i, 0))],
        out_specs=[columns(tokens, tile)] * 2 + [fixed((tokens, width))],
        out_shape=[jax.ShapeDtypeStruct((tokens, hidden), BF)] * 2 + [jax.ShapeDtypeStruct((tokens, width), BF)],
        scratch_shapes=[pltpu.VMEM((tokens, width), F32)],
        cost_estimate=SMALL,
        compiler_params=pltpu.CompilerParams(vmem_limit_bytes=TILE_ROOM),
    )(feed, gate_s, up_s, gate_w, up_w, down_w)


def shards(
    hidden,
    positions,
    input_gain,
    query_weight,
    key_weight,
    value_weight,
    query_gain,
    key_gain,
    out_weight,
    branch_gain,
    middle_gain,
    gate_weight,
    up_weight,
    down_weight,
    final_gain,
    cotangent,
):
    packs, rows, width = hidden.shape
    size = key_weight.shape[1]
    heads = query_weight.shape[1] // size
    tokens = packs * rows
    groups = lax.axis_size(GROUPS)
    count = groups * packs
    head = lax.axis_index("head")
    place = lax.axis_index("quad")
    group = lax.axis_index(GROUPS)
    me = group * packs + place
    far_count = lax.axis_size("far")

    def places_of(*orders):
        return jnp.stack([list_places(order, packs, far_count) for order in orders])

    def as_row(gain):
        return gain.astype(F32).reshape(1, -1)

    gain_input, gain_query, gain_key = as_row(input_gain), as_row(query_gain), as_row(key_gain)
    gain_branch, gain_middle, gain_final = as_row(branch_gain), as_row(middle_gain), as_row(final_gain)

    pieces = to_packs(hidden, place)
    upstream_pieces = to_packs(cotangent, place)
    pack_position = lax.dynamic_slice(positions, (place, 0), (1, 1))[0, 0]
    start = (me * 2 + head) * rows - pack_position
    info = jnp.stack([group, place, head, start]).astype(jnp.int32)
    chips = group * packs + (jnp.arange(packs, dtype=jnp.int32) ^ place)
    firsts = (chips[None, :] * 2 + jnp.arange(2, dtype=jnp.int32)[:, None]) * rows
    token_index = firsts[:, :, None] + jnp.arange(rows, dtype=jnp.int32)
    angles = angles_for(token_index.reshape(2 * tokens) - start, size)
    cosine, sine = jnp.cos(angles), jnp.sin(angles)

    wide = heads * size
    own_tokens, key_raw, pair = whole_call(
        functools.partial(enter_kernel, packs),
        [((tokens, width), BF), ((tokens, size), F32), ((tokens, 2 * size), BF)],
        info,
        *pieces,
        gain_input,
        key_weight,
        value_weight,
        gain_key,
        cosine,
        sine,
    )
    other_tokens = over_head(own_tokens)
    pairs = [pair] + [shifted(pair, step) for step in range(1, groups)]
    tokens_both, normed_both, query_raw, queries = whole_call(
        functools.partial(query_kernel, heads),
        [((2 * tokens, width), BF), ((2 * tokens, width), BF), ((2 * tokens, wide), F32), ((2 * tokens, wide), BF)],
        info,
        own_tokens,
        other_tokens,
        gain_input,
        query_weight,
        gain_query,
        cosine,
        sine,
    )
    part = attend(info, queries, pairs, heads, packs)
    attended, totals, mixed, branch, residual, middle = whole_call(
        functools.partial(branch_kernel, heads),
        [
            ((2 * tokens, wide), F32),
            ((2 * tokens, LANES), F32),
            ((2 * tokens, wide), BF),
            ((2 * tokens, width), F32),
            ((2 * tokens, width), F32),
            ((2 * tokens, width), BF),
        ],
        info,
        part,
        over_head(part),
        tokens_both,
        out_weight,
        gain_branch,
        gain_middle,
    )
    middle, *upstream_pieces = tie(middle, *upstream_pieces)
    own_upstream = jnp.concatenate(upstream_pieces, 0)
    other_upstream = over_head(own_upstream)
    act, gate_s, up_s, feed_part = feed_forward(middle, gate_weight, up_weight, down_weight)
    output, upstream, feed_low, final_gain_sum = whole_call(
        finish_kernel,
        [((tokens, width), BF), ((2 * tokens, width), BF), ((2 * tokens, width), BF), ((1, width), F32)],
        info,
        feed_part,
        over_head(feed_part),
        residual,
        own_upstream,
        other_upstream,
        gain_final,
        scratch=[pltpu.VMEM((2 * tokens, width), F32)],
    )

    half_out = (width // 2 + LANES - 1) // LANES * LANES
    chains = {}
    ends = {}
    env = {}
    token = group

    def lists_of(first_name, left, right, cuts):
        nonlocal token
        names = range(first_name, first_name + len(cuts))
        orders = sorted({ORDERS[name] for name in names})
        route, at = [], 0
        for name, cut in zip(names, cuts):
            route.append((orders.index(ORDERS[name]), at, at + cut))
            at += cut
        found = weight_lists(places_of(*orders), left, right, tuple(route), LIST_TILE)
        token, *flat = tie(token, *sum([list(one) for one in found], []))
        for index, name in enumerate(names):
            steps = ORDERS[name][: STEPS[name]]
            chains[name] = Chain(flat[2 * index : 2 * index + 2], steps, len(steps) == 4)

    def compute_down():
        nonlocal token
        token, left, right = tie(token, feed_low, act)
        lists_of(DOWN, left, right, DOWN_CUTS)

    def compute_back():
        nonlocal token
        token, left = tie(token, feed_low)
        result = feed_back(left, gate_s, up_s, gate_weight, up_weight, down_weight)
        token, env["gate_low"], env["up_low"], env["middle_part"] = tie(token, *result)

    def compute_lists(name, source, cuts):
        nonlocal token
        token, left, right = tie(token, middle, env[source])
        lists_of(name, left, right, cuts)

    def compute_branch():
        nonlocal token
        result = whole_call(
            functools.partial(branch_back_kernel, heads),
            [
                ((2 * tokens, width), F32),
                ((2 * tokens, half_out), BF),
                ((2 * tokens, wide + LANES), BF),
                ((1, width), F32),
                ((1, width), F32),
            ],
            info,
            env["middle_part"],
            env[SEND_MIDDLE],
            residual,
            branch,
            upstream,
            attended,
            totals,
            out_weight,
            gain_middle,
            gain_branch,
        )
        token, *result = tie(token, *result)
        env["residual_grad"], env["branch_half"], env["scaled"], env["middle_gain"], env["branch_gain"] = result

    def compute_attention():
        nonlocal token
        token, scaled = tie(token, env["scaled"])
        token, env["query_part"], pair_part = tie(token, *attend_back(info, queries, scaled, pairs, heads, packs))
        ends[PAIRS] = summed_over(pair_part, GROUPS)

    def compute_out():
        nonlocal token
        token, left, right = tie(token, mixed, env["branch_half"])
        lists = small_lists(places_of(ORDERS[OUT]), left, (right,), ())
        token, *lists = tie(token, *lists)
        chains[OUT] = Chain(lists, ORDERS[OUT])

    def compute_query():
        nonlocal token
        result = whole_call(
            functools.partial(query_back_kernel, heads),
            [((2 * tokens, wide // 2), BF), ((1, size), F32), ((tokens, width), F32)],
            info,
            env["query_part"],
            env[SEND_GRAD],
            query_raw,
            gain_query,
            cosine,
            sine,
            query_weight,
            scratch=[pltpu.VMEM((2 * tokens, wide), BF)],
        )
        token, env["query_half"], env["query_gain"], env["back"] = tie(token, *result)

    def compute_query_lists():
        nonlocal token
        token, right = tie(token, env["query_half"])
        lists = small_lists(places_of(ORDERS[QUERY]), normed_both, (right,), ())
        token, *lists = tie(token, *lists)
        chains[QUERY] = Chain(lists, ORDERS[QUERY])

    def compute_key():
        nonlocal token
        result = whole_call(
            key_back_kernel,
            [((tokens, size), BF), ((tokens, size), BF), ((tokens, 2 * size), BF), ((1, size), F32)],
            info,
            ends[PAIRS],
            key_raw,
            gain_key,
            cosine,
            sine,
        )
        token, env["pair_mine"], env["pair_other"], env["pair_low"], env["key_gain"] = tie(token, *result)

    def compute_in():
        nonlocal token
        block = width // (2 * count)
        small = [env[name].reshape(count, 2, -1) for name in ("query_gain", "key_gain")]
        room = block - 2 * small[0].shape[2]
        small = jnp.concatenate(small + [jnp.zeros((count, 2, room), F32)], 2).reshape(1, width)
        sums = (env["branch_gain"], env["middle_gain"], final_gain_sum, small)
        token, mine = tie(token, env["pair_mine"])
        lists = small_lists(places_of(ORDERS[PAIR]), normed_both, (mine, env[SEND_PAIR]), sums)
        token, *lists = tie(token, *lists)
        chains[PAIR] = Chain(lists, ORDERS[PAIR])

    def compute_input():
        nonlocal token
        token, back = tie(token, env["back"])
        (rows_back,) = whole_call(
            leave_kernel,
            [((tokens, 2 * width), BF)],
            info,
            back,
            env["pair_low"],
            key_weight,
            value_weight,
            own_tokens,
            gain_input,
            env["residual_grad"],
            output,
        )
        token, rows_back = tie(token, rows_back)
        env["input_gradient"] = from_packs(rows_back, packs)

    def by_rows(reduced):
        rows_here = reduced.shape[0] // 2
        mine = lax.dynamic_slice_in_dim(reduced, head * rows_here, rows_here, 0)
        other = over_head(lax.dynamic_slice_in_dim(reduced, (1 - head) * rows_here, rows_here, 0))
        return mine, other

    works = {
        DOWN: compute_down,
        BACK: compute_back,
        GATE: lambda: compute_lists(GATE, "gate_low", GATE_CUTS),
        UP: lambda: compute_lists(UP, "up_low", UP_CUTS),
        BRANCH: compute_branch,
        ATTEND: compute_attention,
        OUT: compute_out,
        QUERY: compute_query,
        QUERY_LISTS: compute_query_lists,
        PAIR: compute_key,
        PAIR_LISTS: compute_in,
        INPUT: compute_input,
    }
    sends = {SEND_MIDDLE: "middle_part", SEND_GRAD: "query_part", SEND_PAIR: "pair_other"}
    flights = {}
    for kind, name in PLAN:
        if kind == WORK:
            works[name]()
        elif kind == SEND:
            token, value = tie(token, env[sends[name]])
            flights[name] = over_head(value)
        elif kind == TAKE and name == INPUT:
            token, *env["input_gradient"] = tie(token, *env["input_gradient"])
        elif kind == TAKE:
            token, env[name] = tie(token, flights[name])
        elif kind == START:
            token = chains[name].start(token)
        elif kind == LAND:
            token = chains[name].land(token)
            if chains[name].rest is None:
                continue
            if name in (OUT, QUERY, PAIR):
                ends[name] = summed_over(chains[name].rest, GROUPS)
            for joint, (sources, steps) in JOINTS.items():
                if joint in chains or joint in ends or any(s not in chains or chains[s].rest is None for s in sources):
                    continue
                total = jnp.concatenate([chains[source].rest for source in sources], 1)
                if steps:
                    token, *lists = tie(token, *halves(total))
                    chains[joint] = Chain(lists, steps, steps[-1] == FAR)
                else:
                    token, total = tie(token, total)
                    ends[joint] = summed_over(total, GROUPS)
        else:
            token, ends[name] = tie(token, ends[name])

    def result(*names):
        return jnp.concatenate([ends[n].astype(F32) if n in ends else chains[n].rest for n in names], 1)

    down_sum, gate_sum, up_sum = result(*DOWN_RESULT), result(*GATE_RESULT), result(*UP_RESULT)
    lower = head == 0

    def in_order(mine, other):
        return jnp.where(lower, mine, other).astype(F32), jnp.where(lower, other, mine).astype(F32)

    first, second = in_order(*by_rows(ends[OUT]))
    out_sum = jnp.concatenate([first, second[:, 2 * half_out - width :]], 1)
    query_sum = jnp.concatenate(in_order(*by_rows(ends[QUERY])), 1)
    mine, other = by_rows(ends[PAIR])
    key_sum, value_sum = in_order(mine[:, :size], other[:, :size])
    sums = mine[:, size:].astype(F32) + other[:, size:].astype(F32)
    rows_here = query_sum.shape[0]
    first_row = (2 * me + head) * rows_here
    token_row = (2 * (token * packs + place) + head) * rows_here
    gain_piece = lax.dynamic_slice_in_dim(gain_input[0], token_row, rows_here, 0)
    input_gain_sum = 0.0
    for weight, gradient in ((query_weight, query_sum), (key_weight, key_sum), (value_weight, value_sum)):
        piece = lax.dynamic_slice_in_dim(weight, first_row, rows_here, 0).astype(F32)
        input_gain_sum = input_gain_sum + jnp.sum(piece * gradient, 1)
    input_gain_sum = input_gain_sum / gain_piece
    few = size // (2 * count)

    rows_back = in_place(env["input_gradient"], place)

    return (
        rows_back[:, :, width:],
        rows_back[:, :, :width].astype(F32),
        input_gain_sum,
        query_sum,
        key_sum,
        value_sum,
        sums[:few, 3],
        sums[few : 2 * few, 3],
        out_sum,
        sums[:, 0],
        sums[:, 1],
        gate_sum,
        up_sum,
        down_sum.T,
        sums[:, 2],
    )


def solution(mesh):
    packs = 4
    split = Mesh(
        mesh.devices.reshape(-1, 2, packs, mesh.shape["head"]), ("far", "near", "quad", "head")
    )
    seq_axes = ("far", "near", "quad")
    all_axes = seq_axes + ("head",)
    tokens = P(None, all_axes, None)
    both = P(all_axes)
    both_rows = P(all_axes, None)
    in_specs = (
        tokens,
        P(None, all_axes),
        P(),
        P(),
        P(),
        P(),
        P(),
        P(),
        P(),
        P(),
        P(),
        P(None, "head"),
        P(None, "head"),
        P("head", None),
        P(),
        tokens,
    )
    out_specs = (
        tokens,
        tokens,
        both,
        both_rows,
        both_rows,
        both_rows,
        both,
        both,
        both_rows,
        both,
        both,
        P(seq_axes, "head"),
        P(seq_axes, "head"),
        P("head", seq_axes),
        both,
    )
    return jax.shard_map(shards, mesh=split, in_specs=in_specs, out_specs=out_specs, check_vma=False)
```
